256 devices in a mesh: dp: 64 (over y, z, core), cand: 4 (over x).
Axes of the slice: x: 4, y: 4, z: 8, core: 2. Of those that a mesh axis runs over, the one named last changes fastest.
Arguments:
- embeddings: bfloat16 [65536, 1024], P('dp')
- point_parent: int32 [65536], P('dp'), may hold values from 0 to 255, as said below
- parent_list: int32 [64, 16], replicated, may hold values from 0 to 255, as said below
- block_slots: int32 [256, 4, 2], replicated, may hold values from 0 to 2047, as said below
- centroids: bfloat16 [2048, 128, 1024], P(('dp', 'cand'))
Outputs:
- new_centroids: bfloat16 [2048, 128, 1024], P(('dp', 'cand'))
- log_partition: float32 [65536], P('dp')
The draws below stay inside these ranges and needn't reach their ends.
Inputs may be any that keep to these rules, and one draw needn't show every extreme that they name: `point_parent`: the rows of one index of dp belong only to the parents of its entry of parent_list and come in the order of that list; each listed parent has 16 to 112 rows there, and one of them exactly 112. `parent_list`: each index of dp lists 16 distinct parents. `block_slots`: every storage block is named once. Block s lies on the device of index s // 8 of dp+cand (dp slowest), and the blocks of quarter q lie on devices whose cand index is q. The 32 blocks of one quarter that the parents of one index of dp name lie on distinct indices of dp.
All inputs are finite; a program needn't handle non-finite values.
Results may differ from the reference program's by a relative error of at most 0.0065.
Values may be sent and summed in bfloat16 or wider, within the bound.
A program may use at most 192 MiB of HBM per device.

```python
import jax
import jax.numpy as jnp
from jax import lax

D = 1024
BLOCK = 128
QB = 2
BPD = 8
TOK_DEV = 1024
PPD = 16
AVG = 64
MAXP = 112
PARENTS = 256
SLOTS = 2048
TOKENS = 65536
N_DP = 64
N_CAND = 4


def layout(key):
    half_count = N_DP // 2
    quarter_keys = jax.random.split(jax.random.fold_in(key, 101), N_CAND)
    owners = jax.vmap(lambda subkey: jax.random.permutation(subkey, N_DP))(quarter_keys)
    parent_ids = jnp.arange(PARENTS, dtype=jnp.int32)
    groups = parent_ids % half_count
    depths = parent_ids // half_count
    pair_ids = QB * groups[:, None] + jnp.arange(QB, dtype=jnp.int32)[None, :]
    owner_dp = jnp.transpose(owners[:, pair_ids], (1, 0, 2))
    quarter_ids = jnp.arange(N_CAND, dtype=jnp.int32)[None, :, None]
    slot_ids = (owner_dp * N_CAND + quarter_ids) * BPD + depths[:, None, None]
    device_keys = jax.random.split(jax.random.fold_in(key, 102), N_DP)
    picked = jax.vmap(lambda subkey: jax.random.permutation(subkey, half_count)[:PPD])(device_keys)
    levels = jax.random.randint(jax.random.fold_in(key, 103), (N_DP, PPD), 0, BPD)
    lists_all = (picked + half_count * levels).astype(jnp.int32)
    smallest = AVG // 4
    former = jax.random.randint(jax.random.fold_in(key, 104), (N_DP, PPD // 2), smallest, MAXP + 1)
    full_pair = jax.random.randint(jax.random.fold_in(key, 105), (N_DP, 1), 0, PPD // 2)
    former = jnp.where(jnp.arange(PPD // 2)[None, :] == full_pair, MAXP, former)
    counts = jnp.stack([former, 2 * AVG - former], axis=2).reshape(N_DP, PPD)
    bounds = jnp.cumsum(counts, axis=1)
    row_ids = jnp.arange(TOK_DEV, dtype=jnp.int32)
    segment = jnp.sum((bounds[:, None, :] <= row_ids[None, :, None]).astype(jnp.int32), axis=2)
    parents = jnp.take_along_axis(lists_all, segment, axis=1).reshape(-1)
    return (slot_ids.astype(jnp.int32), lists_all, parents.astype(jnp.int32))


def draw_point_parent(key, part):
    slot_ids, lists_all, parents = layout(key)
    return parents


def draw_parent_list(key, part):
    slot_ids, lists_all, parents = layout(key)
    return lists_all


def draw_block_slots(key, part):
    slot_ids, lists_all, parents = layout(key)
    return slot_ids


def draw_embeddings(key, part):
    key = jax.random.fold_in(key, 4)
    values = jax.random.normal(key, (TOKENS, D), jnp.float32)
    return values.astype(jnp.bfloat16)


def draw_centroids(key, part):
    key = jax.random.fold_in(key, 5)
    values = jax.random.normal(key, (SLOTS, BLOCK, D), jnp.float32) / 32.0
    return values.astype(jnp.bfloat16)


def setup_inputs(seed: int = 0) -> dict:
    seeds = jax.random.split(jax.random.key(seed), 6)
    embeddings = draw_embeddings(jax.random.fold_in(seeds[5], 71), 0)
    point_parent = draw_point_parent(jax.random.fold_in(seeds[5], 71), 0)
    parent_list = draw_parent_list(jax.random.fold_in(seeds[5], 71), 0)
    block_slots = draw_block_slots(jax.random.fold_in(seeds[5], 71), 0)
    centroids = draw_centroids(jax.random.fold_in(seeds[5], 71), 0)
    return dict(embeddings=embeddings, point_parent=point_parent, parent_list=parent_list, block_slots=block_slots, centroids=centroids)


sharpness = 3.0
prior_mass = 1.0


def reference(embeddings, point_parent, parent_list, block_slots, centroids):
    flat_cent = centroids.reshape(SLOTS * BLOCK, D)
    device_rows = embeddings.reshape(N_DP, TOK_DEV, D)
    device_parents = point_parent.reshape(N_DP, TOK_DEV)
    device_ids = jnp.repeat(jnp.arange(N_DP, dtype=jnp.int32), PPD)
    entry_ids = jnp.tile(jnp.arange(PPD, dtype=jnp.int32), N_DP)
    listing = jnp.arange(PPD, dtype=jnp.int32)
    within = jnp.arange(MAXP, dtype=jnp.int32)
    lane_ids = jnp.arange(BLOCK, dtype=jnp.int32)

    def visit_window(state_now, pieces):
        summed, mass_rows, log_part = state_now
        device, entry_index = pieces
        own_list = parent_list[device]
        parent = own_list[entry_index]
        parents_here = device_parents[device]
        position = jnp.sum(jnp.where(parents_here[:, None] == own_list[None, :], listing[None, :], 0), axis=1)
        first_row = jnp.sum((position < entry_index).astype(jnp.int32))
        first_row = jnp.minimum(first_row, TOK_DEV - MAXP).astype(jnp.int32)
        window = lax.dynamic_slice_in_dim(device_rows[device], first_row, MAXP, 0)
        keep_rows = lax.dynamic_slice_in_dim(position, first_row, MAXP, 0) == entry_index
        slot_ids = block_slots[parent].reshape(-1)
        child_rows = (slot_ids[:, None] * BLOCK + lane_ids[None, :]).reshape(-1).astype(jnp.int32)
        children = jnp.take(flat_cent, child_rows, axis=0)
        scores = jnp.dot(window, children.T, preferred_element_type=jnp.float32)
        squares = jnp.sum(jnp.square(children.astype(jnp.float32)), axis=1)
        logits = sharpness * (scores - 0.5 * squares[None, :])
        highest = jnp.max(logits, axis=1, keepdims=True)
        log_norm = highest[:, 0] + jnp.log(jnp.sum(jnp.exp(logits - highest), axis=1))
        weights = jnp.where(keep_rows[:, None], jnp.exp(logits - log_norm[:, None]), 0.0).astype(jnp.bfloat16)
        summed = summed.at[child_rows].add(jnp.dot(weights.T, window, preferred_element_type=jnp.float32))
        mass_rows = mass_rows.at[child_rows].add(jnp.sum(weights.astype(jnp.float32), axis=0))
        targets = (device * TOK_DEV + first_row + within).astype(jnp.int32)
        log_part = log_part.at[targets].set(jnp.where(keep_rows, log_norm, log_part[targets]))
        return (summed, mass_rows, log_part), None

    initial = (jnp.zeros((SLOTS * BLOCK, D), jnp.float32), jnp.zeros((SLOTS * BLOCK,), jnp.float32), jnp.zeros((TOKENS,), jnp.float32))
    final_state, _ = lax.scan(visit_window, initial, (device_ids, entry_ids))
    summed, mass_rows, log_part = final_state
    updated = (summed + prior_mass * flat_cent.astype(jnp.float32)) / (mass_rows[:, None] + prior_mass)
    return updated.astype(jnp.bfloat16).reshape(SLOTS, BLOCK, D), log_part
```

```python
import functools

import jax
import jax.numpy as jnp
from jax import lax
from jax.experimental import pallas as pl
from jax.experimental.pallas import tpu as pltpu
from jax.sharding import Mesh
from jax.sharding import PartitionSpec as P

sharpness = 3.0
prior_mass = 1.0

GRAIN = 16
SPAN = 8
NY, NZ, NC, NQ = 4, 8, 2, 4
NDP = NY * NZ * NC
PER_Y = NZ * NC
MESH = pl.DeviceIdType.MESH
VMEM_LIMIT = 56 * 2**20


def pack_kernel(count, pick_ref, grains_ref, out_ref):
    target = pl.program_id(0)

    @pl.loop(0, count)
    def _(place):
        out_ref[0, place] = grains_ref[pick_ref[target * count + place]]


def pack(grains, picks):
    targets, count = picks.shape
    shape = grains.shape[1:]
    return pl.pallas_call(
        functools.partial(pack_kernel, count),
        grid_spec=pltpu.PrefetchScalarGridSpec(
            num_scalar_prefetch=1,
            grid=(targets,),
            in_specs=[pl.BlockSpec(grains.shape, lambda t, *_: (0, 0, 0))],
            out_specs=pl.BlockSpec((1, count) + shape, lambda t, *_: (t, 0, 0, 0)),
        ),
        out_shape=jax.ShapeDtypeStruct((targets, count) + shape, grains.dtype),
        compiler_params=pltpu.CompilerParams(vmem_limit_bytes=VMEM_LIMIT),
        cost_estimate=pl.CostEstimate(
            flops=0, bytes_accessed=2 * (grains.size + targets * count * shape[0] * shape[1]), transcendentals=0
        ),
    )(picks.reshape(-1), grains)


def window_rows(rows_ref, spot_ref, window):
    parts = [rows_ref[0, spot_ref[window * SPAN + k]] for k in range(SPAN)]
    return jnp.concatenate(parts, axis=0)


def score_kernel(spot_ref, block_ref, low_ref, high_ref, rows_ref, cent_ref, logit_ref, part_ref, square_ref):
    group = pl.program_id(0)

    @pl.when(group == 0)
    def _():
        @pl.loop(0, cent_ref.shape[0])
        def _(b):
            wide = cent_ref[b].astype(jnp.float32)
            square_ref[b] = jnp.sum(wide * wide, axis=1, keepdims=True)

    @pl.loop(0, PER_Y)
    def _(i):
        window = group * PER_Y + i

        @pl.when(high_ref[window] > low_ref[window])
        def _():
            rows = window_rows(rows_ref, spot_ref, window)
            b = block_ref[window]
            scores = lax.dot_general(
                cent_ref[b], rows, (((1,), (1,)), ((), ())), preferred_element_type=jnp.float32
            )
            logits = sharpness * (scores - 0.5 * square_ref[b])
            highest = jnp.max(logits, axis=0, keepdims=True)
            total = jnp.sum(jnp.exp(logits - highest), axis=0, keepdims=True)
            logit_ref[i] = logits
            part_ref[i] = jnp.concatenate([highest, total], axis=0)

        @pl.when(high_ref[window] <= low_ref[window])
        def _():
            part_ref[i] = jnp.zeros(part_ref.shape[1:], jnp.float32)


def update_kernel(spot_ref, block_ref, low_ref, high_ref, rows_ref, cent_ref, logit_ref, norm_ref, out_ref, sum_ref, mass_ref):
    group = pl.program_id(0)

    @pl.when(group == 0)
    def _():
        sum_ref[...] = jnp.zeros_like(sum_ref)
        mass_ref[...] = jnp.zeros_like(mass_ref)

    @pl.loop(0, PER_Y)
    def _(i):
        window = group * PER_Y + i
        low, high = low_ref[window], high_ref[window]

        @pl.when(high > low)
        def _():
            rows = window_rows(rows_ref, spot_ref, window)
            b = block_ref[window]
            place = lax.broadcasted_iota(jnp.int32, logit_ref.shape[1:], 1)
            keep = (place >= low) & (place < high)
            weights = jnp.where(keep, jnp.exp(logit_ref[i] - norm_ref[i]), 0.0).astype(jnp.bfloat16)
            sum_ref[b] += lax.dot_general(
                weights, rows, (((1,), (0,)), ((), ())), preferred_element_type=jnp.float32
            )
            mass_ref[b] += jnp.sum(weights.astype(jnp.float32), axis=1, keepdims=True)

    @pl.when(group == NY - 1)
    def _():
        @pl.loop(0, cent_ref.shape[0])
        def _(b):
            new = (sum_ref[b] + prior_mass * cent_ref[b].astype(jnp.float32)) / (mass_ref[b] + prior_mass)
            out_ref[b] = new.astype(out_ref.dtype)


def score(rows, spots, block, low, high, centroids):
    stored, lanes, width = centroids.shape
    span = SPAN * GRAIN
    return pl.pallas_call(
        score_kernel,
        grid_spec=pltpu.PrefetchScalarGridSpec(
            num_scalar_prefetch=4,
            grid=(NY,),
            in_specs=[
                pl.BlockSpec((1,) + rows.shape[1:], lambda g, *_: (g, 0, 0, 0)),
                pl.BlockSpec(centroids.shape, lambda g, *_: (0, 0, 0)),
            ],
            out_specs=[
                pl.BlockSpec((PER_Y, lanes, span), lambda g, *_: (g, 0, 0)),
                pl.BlockSpec((PER_Y, 2, span), lambda g, *_: (g, 0, 0)),
            ],
            scratch_shapes=[pltpu.VMEM((stored, lanes, 1), jnp.float32)],
        ),
        out_shape=[
            jax.ShapeDtypeStruct((NDP, lanes, span), jnp.float32),
            jax.ShapeDtypeStruct((NDP, 2, span), jnp.float32),
        ],
        compiler_params=pltpu.CompilerParams(vmem_limit_bytes=VMEM_LIMIT),
        cost_estimate=pl.CostEstimate(
            flops=NDP * lanes * span * width, bytes_accessed=2 * rows.size, transcendentals=NDP * lanes * span
        ),
    )(spots.reshape(-1), block, low, high, rows, centroids)


def update(rows, spots, block, low, high, centroids, logits, norms):
    stored, lanes, width = centroids.shape
    span = SPAN * GRAIN
    return pl.pallas_call(
        update_kernel,
        grid_spec=pltpu.PrefetchScalarGridSpec(
            num_scalar_prefetch=4,
            grid=(NY,),
            in_specs=[
                pl.BlockSpec((1,) + rows.shape[1:], lambda g, *_: (g, 0, 0, 0)),
                pl.BlockSpec(centroids.shape, lambda g, *_: (0, 0, 0)),
                pl.BlockSpec((PER_Y, lanes, span), lambda g, *_: (g, 0, 0)),
                pl.BlockSpec((PER_Y, 1, span), lambda g, *_: (g, 0, 0)),
            ],
            out_specs=pl.BlockSpec(centroids.shape, lambda g, *_: (0, 0, 0)),
            scratch_shapes=[
                pltpu.VMEM((stored, lanes, width), jnp.float32),
                pltpu.VMEM((stored, lanes, 1), jnp.float32),
            ],
        ),
        out_shape=jax.ShapeDtypeStruct(centroids.shape, centroids.dtype),
        compiler_params=pltpu.CompilerParams(vmem_limit_bytes=VMEM_LIMIT),
        cost_estimate=pl.CostEstimate(
            flops=NDP * lanes * span * width, bytes_accessed=2 * rows.size, transcendentals=NDP * lanes * span
        ),
    )(spots.reshape(-1), block, low, high, rows, centroids, logits, norms)


def joint(former, latter):
    highest = jnp.maximum(former[0:1], latter[0:1])
    total = former[1:2] * jnp.exp(former[0:1] - highest) + latter[1:2] * jnp.exp(latter[0:1] - highest)
    return jnp.concatenate([highest, total], axis=0)


def exchange_kernel(
    first_ref, second_ref, pick_ref, part_ref, got_ref, own_ref,
    back_ref, half_ref, quarters_ref, send_ref, land_ref,
    back_send, back_recv, cross_send, cross_recv, fore_send, fore_recv,
):
    y, z, c, q = (lax.axis_index(a) for a in ("y", "z", "core", "cand"))
    here = (y * NZ + z) * NC + c
    listed = own_ref.shape[0]

    def device(index):
        return (index // PER_Y, (index // NC) % NZ, index % NC, q)

    def crossing(step):
        return (y, z, c, (q + step) % NQ)

    barrier = pltpu.get_barrier_semaphore()

    @pl.loop(1, NDP)
    def _(t):
        pl.semaphore_signal(barrier, 1, device_id=device((here + t) % NDP), device_id_type=MESH)

    for step in range(1, NQ):
        pl.semaphore_signal(barrier, 1, device_id=crossing(step), device_id_type=MESH)
    pl.semaphore_wait(barrier, NDP - 1 + NQ - 1)

    def back(t):
        peer = (here + t) % NDP
        return pltpu.make_async_remote_copy(
            part_ref.at[peer], back_ref.at[here], back_send.at[t], back_recv.at[t],
            device_id=device(peer), device_id_type=MESH,
        )

    def fore(t):
        peer = (here + t) % NDP
        return pltpu.make_async_remote_copy(
            send_ref.at[peer], land_ref.at[here], fore_send.at[t], fore_recv.at[t],
            device_id=device(peer), device_id_type=MESH,
        )

    def cross(step):
        return pltpu.make_async_remote_copy(
            half_ref, quarters_ref.at[step], cross_send.at[step], cross_recv.at[step],
            device_id=crossing(step), device_id_type=MESH,
        )

    @pl.loop(1, NDP)
    def _(t):
        back(t).start()

    back_ref[here] = part_ref[here]

    @pl.loop(1, NDP)
    def _(t):
        back(t).wait()

    @pl.loop(0, listed)
    def _(e):
        half_ref[e] = joint(back_ref[first_ref[e]], back_ref[second_ref[e]])

    for step in range(1, NQ):
        cross(step).start()
    for step in range(1, NQ):
        cross(step).wait()

    @pl.loop(0, listed)
    def _(e):
        both = joint(half_ref[e], quarters_ref[1, e])
        rest = joint(quarters_ref[2, e], quarters_ref[3, e])
        pair = joint(both, rest)
        own_ref[e] = pair[0:1] + jnp.log(pair[1:2])

    @pl.loop(0, NDP)
    def _(j):
        send_ref[j] = own_ref[pick_ref[j]]

    @pl.loop(1, NDP)
    def _(t):
        fore(t).start()

    land_ref[here] = send_ref[here]

    @pl.loop(1, NDP)
    def _(t):
        fore(t).wait()

    got_ref[...] = land_ref[...]


def exchange(first, second, pick, part, collective_id):
    listed = first.shape[0]
    span = SPAN * GRAIN
    smem, vmem = pl.BlockSpec(memory_space=pltpu.SMEM), pl.BlockSpec(memory_space=pltpu.VMEM)
    dma = pltpu.SemaphoreType.DMA
    return pl.pallas_call(
        exchange_kernel,
        in_specs=[smem, smem, smem, vmem],
        out_specs=[vmem, vmem],
        out_shape=[
            jax.ShapeDtypeStruct((NDP, 1, span), jnp.float32),
            jax.ShapeDtypeStruct((listed, 1, span), jnp.float32),
        ],
        scratch_shapes=[
            pltpu.VMEM((NDP, 2, span), jnp.float32),
            pltpu.VMEM((listed, 2, span), jnp.float32),
            pltpu.VMEM((NQ, listed, 2, span), jnp.float32),
            pltpu.VMEM((NDP, 1, span), jnp.float32),
            pltpu.VMEM((NDP, 1, span), jnp.float32),
            dma((NDP,)), dma((NDP,)), dma((NQ,)), dma((NQ,)), dma((NDP,)), dma((NDP,)),
        ],
        compiler_params=pltpu.CompilerParams(
            collective_id=collective_id, has_side_effects=True, vmem_limit_bytes=16 * 2**20
        ),
    )(first, second, pick, part)


def on_device(embeddings, point_parent, parent_list, block_slots, centroids):
    y, z, c, q = (lax.axis_index(a) for a in ("y", "z", "core", "cand"))
    here = (y * NZ + z) * NC + c
    row_count, width = embeddings.shape
    stored = centroids.shape[0]
    listed = parent_list.shape[1]
    grains = row_count // GRAIN
    local = grains // NQ
    i32 = jnp.int32

    share = lax.dynamic_index_in_dim(embeddings.reshape(local, NQ, GRAIN, width), q, 1, keepdims=False)
    shares = lax.all_gather(share, "z", axis=0, tiled=True)

    counts = jnp.sum((point_parent[:, None] == parent_list[here][None, :]).astype(i32), axis=0)
    counts = lax.all_gather(counts, ("y", "z", "core"), axis=0)
    starts = jnp.cumsum(counts, axis=1) - counts
    grain0 = starts // GRAIN
    low = starts % GRAIN
    high = low + counts
    slots = jnp.take(block_slots, parent_list, axis=0)
    owner = slots // (stored * NQ)

    mine = jnp.take(owner, q, axis=2) == here
    entry = jnp.any(mine, axis=2)
    chosen = lambda value: jnp.sum(jnp.where(entry, value, 0), axis=1)
    serve_low, serve_high, serve_grain = chosen(low), chosen(high), chosen(grain0)
    serve_block = jnp.sum(jnp.where(mine, jnp.take(slots, q, axis=2) % stored, 0), axis=(1, 2))

    dps = jnp.arange(NDP, dtype=i32)
    own_owner = lax.dynamic_index_in_dim(jnp.take(owner, q, axis=2), here, 0, keepdims=False)
    pick = jnp.sum(
        jnp.where(own_owner[None] == dps[:, None, None], jnp.arange(listed, dtype=i32)[None, :, None], 0), axis=(1, 2)
    )

    def by_place(value):
        return value.reshape((NY, NZ, NC) + value.shape[1:])

    src_owner = lax.dynamic_index_in_dim(by_place(owner), y, 0, keepdims=False)
    src_owner = lax.dynamic_index_in_dim(src_owner, c, 1, keepdims=False)
    src_grain = lax.dynamic_index_in_dim(by_place(grain0), y, 0, keepdims=False)
    src_grain = lax.dynamic_index_in_dim(src_grain, c, 1, keepdims=False)
    target = (jnp.arange(NY, dtype=i32)[:, None] * NZ + z) * NC + jnp.arange(NC, dtype=i32)[None, :]
    hit = jnp.any(src_owner[None, None] == target[:, :, None, None, None, None], axis=-1)
    begin = jnp.sum(jnp.where(hit, src_grain[None, None, :, :, None], 0), axis=3)
    begin = jnp.swapaxes(begin, 2, 3)
    nearest = (begin + (q - begin) % NQ) // NQ
    slot = jnp.arange(2, dtype=i32)
    picks = jnp.minimum(nearest[..., None] + slot, local - 1) + local * jnp.arange(NZ, dtype=i32)[:, None]
    packed = pack(shares, picks.reshape(NY * NC * NQ, NZ * 2))
    rows = lax.all_to_all(packed, ("y", "core", "cand"), split_axis=0, concat_axis=0, tiled=True)
    rows = rows.reshape(NY, NC * NQ * NZ * 2, GRAIN, width)
    step = jnp.arange(SPAN, dtype=i32)
    plane = (serve_grain[:, None] + step) % NQ
    from_core, from_z = (dps % NC)[:, None], ((dps // NC) % NZ)[:, None]
    spots = ((from_core * NQ + plane) * NZ + from_z) * 2 + step // NQ

    logits, part = score(rows, spots, serve_block, serve_low, serve_high, centroids)
    norms, own_norms = exchange(own_owner[:, 0], own_owner[:, 1], pick, part, 1)
    updated = update(rows, spots, serve_block, serve_low, serve_high, centroids, logits, norms)

    own = lambda value: lax.dynamic_index_in_dim(value, here, 0, keepdims=False)
    place = jnp.arange(SPAN * GRAIN, dtype=i32)[None, :]
    keep = (place >= own(low)[:, None]) & (place < own(high)[:, None])
    values = jnp.where(keep, own_norms[:, 0, :], 0.0).reshape(listed * SPAN, GRAIN)
    which = (own(grain0)[:, None] + step).reshape(-1)
    spread = (jnp.arange(grains, dtype=i32)[:, None] == which[None, :]).astype(jnp.float32)
    log_partition = jnp.dot(spread, values, precision=lax.Precision.HIGHEST).reshape(row_count)
    return updated, log_partition


def solution(mesh):
    split = Mesh(mesh.devices.reshape(NY, NZ, NC, NQ), ("y", "z", "core", "cand"))
    dp = ("y", "z", "core")
    every = dp + ("cand",)
    return jax.shard_map(
        on_device,
        mesh=split,
        in_specs=(P(dp, None), P(dp), P(), P(), P(every, None, None)),
        out_specs=(P(every, None, None), P(dp)),
        check_vma=False,
    )
```

```python
import functools

import jax
import jax.numpy as jnp
from jax import lax
from jax.experimental import pallas as pl
from jax.experimental.pallas import tpu as pltpu
from jax.sharding import Mesh
from jax.sharding import PartitionSpec as P

sharpness = 3.0
prior_mass = 1.0

GRAIN = 16
SPAN = 8
NY, NZ, NC, NQ = 4, 8, 2, 4
NDP = NY * NZ * NC
PER_Y = NZ * NC
NF = NY * NC
ABREAST = 2
FULL = 2 * PER_Y
ROOMS = (16, 18, 20, 22, FULL)
STEPS = (
    (1, 1), (3, 3), (1, 3), (3, 1), (0, 1), (0, 3), (1, 0), (3, 0),
    (2, 1), (2, 3), (1, 2), (3, 2), (2, 2), (0, 2), (2, 0),
)
MESH = pl.DeviceIdType.MESH
VMEM_LIMIT = 56 * 2**20


def dispatch_kernel(room, pick_ref, grains_ref, rows_ref, send_ref, send_sem, recv_sem, own_sem):
    y, z, c, q = (lax.axis_index(a) for a in ("y", "z", "core", "cand"))
    here = y * NQ + q

    def target(step):
        ty, tq = (y + step[0]) % NY, (q + step[1]) % NQ
        return ty * NQ + tq, (ty, z, c, tq)

    barrier = pltpu.get_barrier_semaphore()
    for step in STEPS:
        pl.semaphore_signal(barrier, 1, device_id=target(step)[1], device_id_type=MESH)
    pl.semaphore_wait(barrier, len(STEPS))

    def copy(n, places):
        index, device = target(STEPS[n])
        return pltpu.make_async_remote_copy(
            send_ref.at[index, places], rows_ref.at[here, places], send_sem.at[n], recv_sem.at[n],
            device_id=device, device_id_type=MESH,
        )

    @pl.loop(0, room)
    def _(place):
        for n, step in enumerate(STEPS):
            index, _ = target(step)
            send_ref[index, place] = grains_ref[pick_ref[index * FULL + place]]
            copy(n, pl.ds(place, 1)).start()
        send_ref[here, place] = grains_ref[pick_ref[here * FULL + place]]

    every = pl.ds(0, room)
    kept = pltpu.make_async_copy(send_ref.at[here, every], rows_ref.at[here, every], own_sem)
    kept.start()
    kept.wait()
    for n in range(len(STEPS)):
        copy(n, every).wait()


def dispatch(room, collective_id, grains, picks):
    targets = picks.shape[0]
    shape = grains.shape[1:]
    return pl.pallas_call(
        functools.partial(dispatch_kernel, room),
        in_specs=[pl.BlockSpec(memory_space=pltpu.SMEM), pl.BlockSpec(memory_space=pltpu.VMEM)],
        out_specs=pl.BlockSpec(memory_space=pl.ANY),
        out_shape=jax.ShapeDtypeStruct((targets, FULL) + shape, grains.dtype),
        scratch_shapes=[
            pltpu.VMEM((targets, room) + shape, grains.dtype),
            pltpu.SemaphoreType.DMA((len(STEPS),)),
            pltpu.SemaphoreType.DMA((len(STEPS),)),
            pltpu.SemaphoreType.DMA,
        ],
        compiler_params=pltpu.CompilerParams(
            collective_id=collective_id, has_side_effects=True, vmem_limit_bytes=VMEM_LIMIT
        ),
        cost_estimate=pl.CostEstimate(
            flops=0, bytes_accessed=2 * (grains.size + targets * room * shape[0] * shape[1]), transcendentals=0
        ),
    )(picks.reshape(-1), grains)


def window_rows(rows_ref, spot_ref, window):
    parts = [rows_ref[0, spot_ref[window * SPAN + k]] for k in range(SPAN)]
    return jnp.concatenate(parts, axis=0)


def by_core(i):
    return (i % NC) * NZ + i // NC


def score_kernel(spot_ref, block_ref, order_ref, many_ref, rows_ref, cent_ref, logit_ref, part_ref, square_ref):
    group = pl.program_id(0)

    @pl.when(group == 0)
    def _():
        @pl.loop(0, cent_ref.shape[0])
        def _(b):
            wide = cent_ref[b].astype(jnp.float32)
            square_ref[b] = jnp.sum(wide * wide, axis=1, keepdims=True)

    @pl.loop(0, (many_ref[group] + ABREAST - 1) // ABREAST)
    def _(step):
        places = [order_ref[group * PER_Y + step * ABREAST + n] for n in range(ABREAST)]
        results = []
        for i in places:
            window = group * PER_Y + i
            rows = window_rows(rows_ref, spot_ref, window)
            b = block_ref[window]
            scores = lax.dot_general(
                cent_ref[b], rows, (((1,), (1,)), ((), ())), preferred_element_type=jnp.float32
            )
            logits = sharpness * (scores - 0.5 * square_ref[b])
            highest = jnp.max(logits, axis=0, keepdims=True)
            total = jnp.sum(jnp.exp(logits - highest), axis=0, keepdims=True)
            results.append((logits, jnp.concatenate([highest, total], axis=0)))
        for i, (logits, part) in zip(places, results):
            logit_ref[i] = logits
            part_ref[by_core(i)] = part


def update_kernel(
    spot_ref, block_ref, low_ref, high_ref, order_ref, many_ref,
    rows_ref, cent_ref, logit_ref, norm_ref, out_ref, sum_ref, mass_ref,
):
    group = pl.program_id(0)

    @pl.when(group == 0)
    def _():
        sum_ref[...] = jnp.zeros_like(sum_ref)
        mass_ref[...] = jnp.zeros_like(mass_ref)

    @pl.loop(0, (many_ref[group] + ABREAST - 1) // ABREAST)
    def _(step):
        results = []
        for n in range(ABREAST):
            i = order_ref[group * PER_Y + step * ABREAST + n]
            window = group * PER_Y + i
            rows = window_rows(rows_ref, spot_ref, window)
            place = lax.broadcasted_iota(jnp.int32, logit_ref.shape[1:], 1)
            keep = (place >= low_ref[window]) & (place < high_ref[window])
            weights = jnp.where(keep, jnp.exp(logit_ref[i] - norm_ref[by_core(i)]), 0.0).astype(jnp.bfloat16)
            sums = lax.dot_general(weights, rows, (((1,), (0,)), ((), ())), preferred_element_type=jnp.float32)
            mass = jnp.sum(weights.astype(jnp.float32), axis=1, keepdims=True)
            results.append((block_ref[window], sums, mass))
        for b, sums, mass in results:
            sum_ref[b] += sums
            mass_ref[b] += mass

    @pl.when(group == NY - 1)
    def _():
        @pl.loop(0, cent_ref.shape[0])
        def _(b):
            new = (sum_ref[b] + prior_mass * cent_ref[b].astype(jnp.float32)) / (mass_ref[b] + prior_mass)
            out_ref[b] = new.astype(out_ref.dtype)


def score(rows, spots, serving, centroids):
    stored, lanes, width = centroids.shape
    span = SPAN * GRAIN
    block, _, _, order, many = serving
    return pl.pallas_call(
        score_kernel,
        grid_spec=pltpu.PrefetchScalarGridSpec(
            num_scalar_prefetch=4,
            grid=(NY,),
            in_specs=[
                pl.BlockSpec((1,) + rows.shape[1:], lambda g, *_: (g, 0, 0, 0)),
                pl.BlockSpec(centroids.shape, lambda g, *_: (0, 0, 0)),
            ],
            out_specs=[
                pl.BlockSpec((PER_Y, lanes, span), lambda g, *_: (g, 0, 0)),
                pl.BlockSpec((PER_Y, 2, span), lambda g, *_: (g, 0, 0)),
            ],
            scratch_shapes=[pltpu.VMEM((stored, lanes, 1), jnp.float32)],
        ),
        out_shape=[
            jax.ShapeDtypeStruct((NDP, lanes, span), jnp.float32),
            jax.ShapeDtypeStruct((NDP, 2, span), jnp.float32),
        ],
        compiler_params=pltpu.CompilerParams(vmem_limit_bytes=VMEM_LIMIT),
        cost_estimate=pl.CostEstimate(
            flops=NDP * lanes * span * width, bytes_accessed=2 * rows.size, transcendentals=NDP * lanes * span
        ),
    )(spots.reshape(-1), block, order, many, rows, centroids)


def update(rows, spots, serving, centroids, logits, norms):
    stored, lanes, width = centroids.shape
    span = SPAN * GRAIN
    return pl.pallas_call(
        update_kernel,
        grid_spec=pltpu.PrefetchScalarGridSpec(
            num_scalar_prefetch=6,
            grid=(NY,),
            in_specs=[
                pl.BlockSpec((1,) + rows.shape[1:], lambda g, *_: (g, 0, 0, 0)),
                pl.BlockSpec(centroids.shape, lambda g, *_: (0, 0, 0)),
                pl.BlockSpec((PER_Y, lanes, span), lambda g, *_: (g, 0, 0)),
                pl.BlockSpec((PER_Y, 1, span), lambda g, *_: (g, 0, 0)),
            ],
            out_specs=pl.BlockSpec(centroids.shape, lambda g, *_: (0, 0, 0)),
            scratch_shapes=[
                pltpu.VMEM((stored, lanes, width), jnp.float32),
                pltpu.VMEM((stored, lanes, 1), jnp.float32),
            ],
        ),
        out_shape=jax.ShapeDtypeStruct(centroids.shape, centroids.dtype),
        compiler_params=pltpu.CompilerParams(vmem_limit_bytes=VMEM_LIMIT),
        cost_estimate=pl.CostEstimate(
            flops=NDP * lanes * span * width, bytes_accessed=2 * rows.size, transcendentals=NDP * lanes * span
        ),
    )(spots.reshape(-1), *serving, rows, centroids, logits, norms)


def joint(former, latter):
    highest = jnp.maximum(former[0:1], latter[0:1])
    total = former[1:2] * jnp.exp(former[0:1] - highest) + latter[1:2] * jnp.exp(latter[0:1] - highest)
    return jnp.concatenate([highest, total], axis=0)


def exchange_kernel(
    first_ref, second_ref, pick_ref, part_ref, got_ref, own_ref,
    flat_ref, deep_ref, half_ref, quarters_ref, send_ref, fore_ref, land_ref,
    send_sem, recv_sem,
):
    y, z, c, q = (lax.axis_index(a) for a in ("y", "z", "core", "cand"))
    flat = y * NC + c
    listed = own_ref.shape[0]

    def across(step):
        peer = (flat + step) % NF
        return peer, (peer // NC, z, peer % NC, q)

    def along(step):
        peer = (z + step) % NZ
        return peer, (y, peer, c, q)

    def crossing(step):
        return (y, z, c, (q + step) % NQ)

    def start(kind, step, source, target, device):
        copy = pltpu.make_async_remote_copy(
            source, target, send_sem.at[kind, step], recv_sem.at[kind, step], device_id=device, device_id_type=MESH
        )
        copy.start()
        return copy

    barrier = pltpu.get_barrier_semaphore()
    for step in range(1, NF):
        pl.semaphore_signal(barrier, 1, device_id=across(step)[1], device_id_type=MESH)
    for step in range(1, NZ):
        pl.semaphore_signal(barrier, 1, device_id=along(step)[1], device_id_type=MESH)
    for step in range(1, NQ):
        pl.semaphore_signal(barrier, 1, device_id=crossing(step), device_id_type=MESH)
    pl.semaphore_wait(barrier, NF - 1 + NZ - 1 + NQ - 1)

    copies = []
    for step in range(1, NF):
        peer, device = across(step)
        copies.append(start(0, step, part_ref.at[peer], flat_ref.at[:, flat], device))
    flat_ref[:, flat] = part_ref[flat]
    for copy in copies:
        copy.wait()
    copies = []
    for step in range(1, NZ):
        peer, device = along(step)
        copies.append(start(1, step, flat_ref.at[peer], deep_ref.at[z], device))
    deep_ref[z] = flat_ref[z]
    for copy in copies:
        copy.wait()

    for e in range(listed):
        one, two = first_ref[e], second_ref[e]
        half_ref[e] = joint(deep_ref[one // NF, one % NF], deep_ref[two // NF, two % NF])
    copies = [start(2, step, half_ref, quarters_ref.at[step], crossing(step)) for step in range(1, NQ)]
    for copy in copies:
        copy.wait()
    for e in range(listed):
        both = joint(half_ref[e], quarters_ref[1, e])
        rest = joint(quarters_ref[2, e], quarters_ref[3, e])
        pair = joint(both, rest)
        own_ref[e] = pair[0:1] + jnp.log(pair[1:2])

    for zj in range(NZ):
        for fj in range(NF):
            send_ref[zj, fj] = own_ref[pick_ref[zj * NF + fj]]
    copies = []
    for step in range(1, NZ):
        peer, device = along(step)
        copies.append(start(3, step, send_ref.at[peer], fore_ref.at[:, z], device))
    fore_ref[:, z] = send_ref[z]
    for copy in copies:
        copy.wait()
    copies = []
    for step in range(1, NF):
        peer, device = across(step)
        copies.append(start(4, step, fore_ref.at[peer], land_ref.at[flat], device))
    land_ref[flat] = fore_ref[flat]
    for copy in copies:
        copy.wait()
    got_ref[...] = land_ref[...]


def exchange(first, second, pick, part, collective_id):
    listed = first.shape[0]
    span = SPAN * GRAIN
    smem, vmem = pl.BlockSpec(memory_space=pltpu.SMEM), pl.BlockSpec(memory_space=pltpu.VMEM)
    buffer = lambda *shape: pltpu.VMEM(shape + (span,), jnp.float32)
    got, own = pl.pallas_call(
        exchange_kernel,
        in_specs=[smem, smem, smem, vmem],
        out_specs=[vmem, vmem],
        out_shape=[
            jax.ShapeDtypeStruct((NF, NZ, 1, span), jnp.float32),
            jax.ShapeDtypeStruct((listed, 1, span), jnp.float32),
        ],
        scratch_shapes=[
            buffer(NZ, NF, 2), buffer(NZ, NF, 2), buffer(listed, 2), buffer(NQ, listed, 2),
            buffer(NZ, NF, 1), buffer(NF, NZ, 1), buffer(NF, NZ, 1),
            pltpu.SemaphoreType.DMA((5, NZ)), pltpu.SemaphoreType.DMA((5, NZ)),
        ],
        compiler_params=pltpu.CompilerParams(
            collective_id=collective_id, has_side_effects=True, vmem_limit_bytes=16 * 2**20
        ),
    )(first, second, pick, part.reshape(NF, NZ, 2, span))
    return got.reshape(NDP, 1, span), own


def on_device(embeddings, point_parent, parent_list, block_slots, centroids):
    y, z, c, q = (lax.axis_index(a) for a in ("y", "z", "core", "cand"))
    here = (y * NZ + z) * NC + c
    row_count, width = embeddings.shape
    stored = centroids.shape[0]
    listed = parent_list.shape[1]
    grains = row_count // GRAIN
    local = grains // NQ
    i32 = jnp.int32

    share = lax.dynamic_index_in_dim(embeddings.reshape(local, NQ, GRAIN, width), q, 1, keepdims=False)
    shares = lax.all_gather(share, ("z", "core"), axis=0, tiled=True)

    counts = jnp.sum((point_parent[:, None] == parent_list[here][None, :]).astype(i32), axis=0)
    counts = lax.all_gather(counts, ("y", "z", "core"), axis=0)
    starts = jnp.cumsum(counts, axis=1) - counts
    begin = starts // GRAIN
    last = (starts + counts - 1) // GRAIN
    low = starts % GRAIN
    high = low + counts
    slots = jnp.take(block_slots, parent_list, axis=0)
    owner = slots // (stored * NQ)
    planes = jnp.arange(NQ, dtype=i32)

    def share_of(begin, last, plane):
        nearest = begin + (plane - begin) % NQ
        return nearest, (nearest <= last).astype(i32) + (nearest + NQ <= last).astype(i32)

    loads = share_of(begin[..., None], last[..., None], planes)[1]
    loads = jnp.broadcast_to(loads[:, :, None, :], (NDP, listed, 2, NQ)).reshape(NY, PER_Y * listed * 2, NQ)
    takers = jnp.swapaxes(owner, 2, 3).reshape(NY, PER_Y * listed * 2, NQ)
    takes = takers[..., None] == jnp.arange(NDP, dtype=i32)
    totals = jnp.einsum(
        "ymqj,ymp->yqjp", takes.astype(jnp.bfloat16), loads.astype(jnp.bfloat16), preferred_element_type=jnp.float32
    )
    size = jnp.sum((jnp.max(totals) > jnp.asarray(ROOMS[:-1], jnp.float32)).astype(i32))

    mine = jnp.take(owner, q, axis=2) == here
    entry = jnp.any(mine, axis=2)
    chosen = lambda value: jnp.sum(jnp.where(entry, value, 0), axis=1)
    served = jnp.any(entry, axis=1)
    serve_low, serve_high, serve_begin = chosen(low), chosen(high), chosen(begin)
    serve_last = jnp.where(served, chosen(last), -1)
    serve_block = jnp.sum(jnp.where(mine, jnp.take(slots, q, axis=2) % stored, 0), axis=(1, 2))
    grouped = served.reshape(NY, PER_Y).astype(i32)
    many = jnp.sum(grouped, axis=1)
    rank = jnp.where(
        grouped > 0, jnp.cumsum(grouped, axis=1) - 1, many[:, None] + jnp.cumsum(1 - grouped, axis=1) - 1
    )
    around = jnp.arange(PER_Y, dtype=i32)
    order = jnp.sum(jnp.where(rank[:, :, None] == around, around[None, :, None], 0), axis=1).reshape(-1)
    serving = (serve_block, serve_low, serve_high, order, many)

    _, landing = share_of(serve_begin[:, None], serve_last[:, None], planes)
    landing = landing.reshape(NY, PER_Y, NQ)
    base = (jnp.cumsum(landing, axis=1) - landing).reshape(NDP, NQ)
    step = jnp.arange(SPAN, dtype=i32)
    grain = serve_begin[:, None] + step
    plane = grain % NQ
    within = jnp.sum(jnp.where(plane[..., None] == planes, base[:, None, :], 0), axis=2) + step // NQ
    real = grain <= serve_last[:, None]
    within = jnp.where(real, within, within[:, :1])
    plane = jnp.where(real, plane, plane[:, :1])
    within = jnp.where(served[:, None], within, 0)

    own = lambda value: lax.dynamic_index_in_dim(value, here, 0, keepdims=False)
    dps = jnp.arange(NDP, dtype=i32)
    by_layer = dps.reshape(NY, NZ, NC).transpose(1, 0, 2).reshape(-1)
    own_owner = own(jnp.take(owner, q, axis=2))
    pick = jnp.sum(
        jnp.where(own_owner[None] == by_layer[:, None, None], jnp.arange(listed, dtype=i32)[None, :, None], 0),
        axis=(1, 2),
    )
    deep = lambda index: (index // NC % NZ) * NF + (index // PER_Y) * NC + index % NC

    of_y = lambda value: lax.dynamic_index_in_dim(value.reshape((NY, PER_Y) + value.shape[1:]), y, 0, keepdims=False)
    target = (jnp.arange(NY, dtype=i32) * NZ + z) * NC + c
    hit = jnp.any(of_y(owner)[None] == target[:, None, None, None, None], axis=-1)
    sent = lambda value: jnp.sum(jnp.where(hit, of_y(value)[None, :, :, None], 0), axis=2)
    nearest, sending = share_of(sent(begin), jnp.where(jnp.any(hit, axis=2), sent(last), -1), q)
    place = jnp.cumsum(sending, axis=1) - sending
    room = jnp.arange(FULL, dtype=i32)
    picks = 0
    for slot in range(2):
        here_now = (place[..., None] + slot == room) & (sending[..., None] > slot)
        which = around[:, None] * local + nearest // NQ + slot
        picks = picks + jnp.sum(jnp.where(here_now, which[..., None], 0), axis=1)
    picks = picks.reshape(NY * NQ, FULL)

    branches = [functools.partial(dispatch, room, 2 + n) for n, room in enumerate(ROOMS)]
    rows = lax.switch(size, branches, shares, picks)
    rows = rows.reshape(NY, NQ * FULL, GRAIN, width)
    spots = plane * FULL + within
    logits, part = score(rows, spots, serving, centroids)
    norms, own_norms = exchange(deep(own_owner[:, 0]), deep(own_owner[:, 1]), pick, part, 1)
    updated = update(rows, spots, serving, centroids, logits, norms)

    place = jnp.arange(SPAN * GRAIN, dtype=i32)[None, :]
    keep = (place >= own(low)[:, None]) & (place < own(high)[:, None])
    values = jnp.where(keep, own_norms[:, 0, :], 0.0).reshape(listed * SPAN, GRAIN)
    which = (own(begin)[:, None] + step).reshape(-1)
    spread = (jnp.arange(grains, dtype=i32)[:, None] == which[None, :]).astype(jnp.float32)
    log_partition = jnp.dot(spread, values, precision=lax.Precision.HIGHEST).reshape(row_count)
    return updated, log_partition


def solution(mesh):
    split = Mesh(mesh.devices.reshape(NY, NZ, NC, NQ), ("y", "z", "core", "cand"))
    dp = ("y", "z", "core")
    every = dp + ("cand",)
    return jax.shard_map(
        on_device,
        mesh=split,
        in_specs=(P(dp, None), P(dp), P(), P(), P(every, None, None)),
        out_specs=(P(every, None, None), P(dp)),
        check_vma=False,
    )
```

```python
import functools

import jax
import jax.numpy as jnp
from jax import lax
from jax.experimental import pallas as pl
from jax.experimental.pallas import tpu as pltpu
from jax.sharding import Mesh
from jax.sharding import PartitionSpec as P

sharpness = 3.0
prior_mass = 1.0

GRAIN = 16
SPAN = 8
NY, NZ, NC, NQ = 4, 8, 2, 4
NDP = NY * NZ * NC
PER_Y = NZ * NC
ABREAST = 4
FULL = 2 * PER_Y
ROOMS = (16, 17, 18, 19, 20, 21, 23, FULL)
STEPS = (
    (1, 1), (3, 3), (1, 3), (3, 1), (0, 1), (0, 3), (1, 0), (3, 0),
    (2, 1), (2, 3), (1, 2), (3, 2), (2, 2), (0, 2), (2, 0),
)
PIECES = (0, 16, 18, 20, 23, FULL)
MESH = pl.DeviceIdType.MESH
VMEM_LIMIT = 56 * 2**20


def dispatch_kernel(room, pick_ref, share_ref, rows_ref, grains_ref, send_ref, send_sem, recv_sem, own_sem):
    y, z, c, q = (lax.axis_index(a) for a in ("y", "z", "core", "cand"))
    here = y * NQ + q

    def target(step):
        ty, tq = (y + step[0]) % NY, (q + step[1]) % NQ
        return ty * NQ + tq, (ty, z, c, tq)

    load = pltpu.make_async_copy(share_ref, grains_ref, own_sem.at[0])
    load.start()
    barrier = pltpu.get_barrier_semaphore()
    for step in STEPS:
        pl.semaphore_signal(barrier, 1, device_id=target(step)[1], device_id_type=MESH)
    pl.semaphore_wait(barrier, len(STEPS))
    load.wait()

    def copy(n, places):
        index, device = target(STEPS[n])
        return pltpu.make_async_remote_copy(
            send_ref.at[index, places], rows_ref.at[here, places], send_sem.at[n], recv_sem.at[n],
            device_id=device, device_id_type=MESH,
        )

    @pl.loop(0, room)
    def _(place):
        for n, step in enumerate(STEPS):
            index, _ = target(step)
            send_ref[index, place] = grains_ref[pick_ref[index * FULL + place]]
            copy(n, pl.ds(place, 1)).start()
        send_ref[here, place] = grains_ref[pick_ref[here * FULL + place]]

    every = pl.ds(0, room)
    kept = pltpu.make_async_copy(send_ref.at[here, every], rows_ref.at[here, every], own_sem.at[1])
    kept.start()
    for n in range(len(STEPS)):
        copy(n, every).wait()
    kept.wait()


def dispatch(room, collective_id, grains, picks):
    targets = picks.shape[0]
    shape = grains.shape[1:]
    return pl.pallas_call(
        functools.partial(dispatch_kernel, room),
        in_specs=[pl.BlockSpec(memory_space=pltpu.SMEM), pl.BlockSpec(memory_space=pl.ANY)],
        out_specs=pl.BlockSpec(memory_space=pl.ANY),
        out_shape=jax.ShapeDtypeStruct((targets, FULL) + shape, grains.dtype),
        scratch_shapes=[
            pltpu.VMEM(grains.shape, grains.dtype),
            pltpu.VMEM((targets, room) + shape, grains.dtype),
            pltpu.SemaphoreType.DMA((len(STEPS),)),
            pltpu.SemaphoreType.DMA((len(STEPS),)),
            pltpu.SemaphoreType.DMA((2,)),
        ],
        compiler_params=pltpu.CompilerParams(
            collective_id=collective_id, has_side_effects=True, vmem_limit_bytes=VMEM_LIMIT
        ),
        cost_estimate=pl.CostEstimate(
            flops=0, bytes_accessed=2 * (grains.size + targets * room * shape[0] * shape[1]), transcendentals=0
        ),
    )(picks.reshape(-1), grains)


def by_core(i):
    return (i % NC) * NZ + i // NC


def fetch(room_ref, rows_ref, held_ref, sems, group, act):
    for n, (begin, end) in enumerate(zip(PIECES, PIECES[1:])):
        places = pl.ds(begin, end - begin)

        @pl.when(room_ref[0] > begin)
        def _():
            act(
                pltpu.make_async_copy(
                    rows_ref.at[group, :, places], held_ref.at[group, :, places], sems.at[group, n]
                )
            )


def window_rows(held_ref, spot_ref, group, window):
    spots = [spot_ref[window * SPAN + k] for k in range(SPAN)]
    return jnp.concatenate([held_ref[group, spot // FULL, spot % FULL] for spot in spots], axis=0)


def score_kernel(
    spot_ref, block_ref, order_ref, many_ref, room_ref, rows_ref, cent_ref, logit_ref, part_ref,
    held_ref, kept_ref, square_ref, in_sem, out_sem,
):
    for group in range(NY):
        fetch(room_ref, rows_ref, held_ref, in_sem, group, lambda copy: copy.start())

    @pl.loop(0, cent_ref.shape[0])
    def _(b):
        wide = cent_ref[b].astype(jnp.float32)
        square_ref[b] = jnp.sum(wide * wide, axis=1, keepdims=True)

    def out(group):
        windows = pl.ds(group * PER_Y, PER_Y)
        return pltpu.make_async_copy(kept_ref.at[windows], logit_ref.at[windows], out_sem.at[group])

    for group in range(NY):
        fetch(room_ref, rows_ref, held_ref, in_sem, group, lambda copy: copy.wait())

        @pl.loop(0, (many_ref[group] + ABREAST - 1) // ABREAST)
        def _(step):
            places = [order_ref[group * PER_Y + step * ABREAST + n] for n in range(ABREAST)]
            results = []
            for i in places:
                window = group * PER_Y + i
                rows = window_rows(held_ref, spot_ref, group, window)
                b = block_ref[window]
                scores = lax.dot_general(
                    cent_ref[b], rows, (((1,), (1,)), ((), ())), preferred_element_type=jnp.float32
                )
                logits = sharpness * (scores - 0.5 * square_ref[b])
                highest = jnp.max(logits, axis=0, keepdims=True)
                total = jnp.sum(jnp.exp(logits - highest), axis=0, keepdims=True)
                results.append((logits, jnp.concatenate([highest, total], axis=0)))
            for i, (logits, part) in zip(places, results):
                kept_ref[group * PER_Y + i] = logits
                part_ref[group * PER_Y + by_core(i)] = part

        out(group).start()
    for group in range(NY):
        out(group).wait()


def update_kernel(
    spot_ref, block_ref, low_ref, high_ref, order_ref, many_ref, room_ref,
    rows_ref, cent_ref, logit_ref, norm_ref, out_ref,
    held_ref, kept_ref, sum_ref, mass_ref, done_ref, in_sem, kept_sem, out_sem,
):
    def kept(group):
        windows = pl.ds(group * PER_Y, PER_Y)
        return pltpu.make_async_copy(logit_ref.at[windows], kept_ref.at[windows], kept_sem.at[group])

    for group in range(NY):
        fetch(room_ref, rows_ref, held_ref, in_sem, group, lambda copy: copy.start())
        kept(group).start()

    sum_ref[...] = jnp.zeros_like(sum_ref)
    mass_ref[...] = jnp.zeros_like(mass_ref)

    for group in range(NY):
        fetch(room_ref, rows_ref, held_ref, in_sem, group, lambda copy: copy.wait())
        kept(group).wait()

        @pl.loop(0, (many_ref[group] + ABREAST - 1) // ABREAST)
        def _(step):
            results = []
            for n in range(ABREAST):
                i = order_ref[group * PER_Y + step * ABREAST + n]
                window = group * PER_Y + i
                rows = window_rows(held_ref, spot_ref, group, window)
                place = lax.broadcasted_iota(jnp.int32, kept_ref.shape[1:], 1)
                keep = (place >= low_ref[window]) & (place < high_ref[window])
                norm = norm_ref[group * PER_Y + by_core(i)]
                weights = jnp.where(keep, jnp.exp(kept_ref[window] - norm), 0.0).astype(jnp.bfloat16)
                sums = lax.dot_general(weights, rows, (((1,), (0,)), ((), ())), preferred_element_type=jnp.float32)
                mass = jnp.sum(weights.astype(jnp.float32), axis=1, keepdims=True)
                results.append((block_ref[window], sums, mass))
            for b, sums, mass in results:
                sum_ref[b] += sums
                mass_ref[b] += mass

    def out(b):
        return pltpu.make_async_copy(done_ref.at[b], out_ref.at[b], out_sem.at[b])

    stored = cent_ref.shape[0]
    for b in range(stored):
        new = (sum_ref[b] + prior_mass * cent_ref[b].astype(jnp.float32)) / (mass_ref[b] + prior_mass)
        done_ref[b] = new.astype(done_ref.dtype)
        out(b).start()
    for b in range(stored):
        out(b).wait()


def score(rows, spots, serving, room, centroids):
    stored, lanes, width = centroids.shape
    span = SPAN * GRAIN
    block, _, _, order, many = serving
    smem, vmem = pl.BlockSpec(memory_space=pltpu.SMEM), pl.BlockSpec(memory_space=pltpu.VMEM)
    return pl.pallas_call(
        score_kernel,
        in_specs=[smem] * 5 + [pl.BlockSpec(memory_space=pl.ANY), vmem],
        out_specs=[pl.BlockSpec(memory_space=pl.ANY), vmem],
        out_shape=[
            jax.ShapeDtypeStruct((NDP, lanes, span), jnp.float32),
            jax.ShapeDtypeStruct((NDP, 2, span), jnp.float32),
        ],
        scratch_shapes=[
            pltpu.VMEM(rows.shape, rows.dtype),
            pltpu.VMEM((NDP, lanes, span), jnp.float32),
            pltpu.VMEM((stored, lanes, 1), jnp.float32),
            pltpu.SemaphoreType.DMA((NY, len(PIECES) - 1)),
            pltpu.SemaphoreType.DMA((NY,)),
        ],
        compiler_params=pltpu.CompilerParams(vmem_limit_bytes=VMEM_LIMIT),
        cost_estimate=pl.CostEstimate(
            flops=NDP * lanes * span * width, bytes_accessed=2 * rows.size, transcendentals=NDP * lanes * span
        ),
    )(spots.reshape(-1), block, order, many, room, rows, centroids)


def update(rows, spots, serving, room, centroids, logits, norms):
    stored, lanes, width = centroids.shape
    span = SPAN * GRAIN
    smem, vmem = pl.BlockSpec(memory_space=pltpu.SMEM), pl.BlockSpec(memory_space=pltpu.VMEM)
    hbm = pl.BlockSpec(memory_space=pl.ANY)
    return pl.pallas_call(
        update_kernel,
        in_specs=[smem] * 7 + [hbm, vmem, hbm, vmem],
        out_specs=hbm,
        out_shape=jax.ShapeDtypeStruct(centroids.shape, centroids.dtype),
        scratch_shapes=[
            pltpu.VMEM(rows.shape, rows.dtype),
            pltpu.VMEM((NDP, lanes, span), jnp.float32),
            pltpu.VMEM((stored, lanes, width), jnp.float32),
            pltpu.VMEM((stored, lanes, 1), jnp.float32),
            pltpu.VMEM(centroids.shape, centroids.dtype),
            pltpu.SemaphoreType.DMA((NY, len(PIECES) - 1)),
            pltpu.SemaphoreType.DMA((NY,)),
            pltpu.SemaphoreType.DMA((stored,)),
        ],
        compiler_params=pltpu.CompilerParams(vmem_limit_bytes=VMEM_LIMIT),
        cost_estimate=pl.CostEstimate(
            flops=NDP * lanes * span * width, bytes_accessed=2 * rows.size, transcendentals=NDP * lanes * span
        ),
    )(spots.reshape(-1), *serving, room, rows, centroids, logits, norms)


def joint(former, latter):
    highest = jnp.maximum(former[0:1], latter[0:1])
    total = former[1:2] * jnp.exp(former[0:1] - highest) + latter[1:2] * jnp.exp(latter[0:1] - highest)
    return jnp.concatenate([highest, total], axis=0)


def plane_peers(y, z, c):
    ys = [lax.rem(y + d, NY) for d in range(NY)]
    zs = [lax.rem(z + d, NZ) for d in range(NZ)]
    cs = [lax.rem(c + d, NC) for d in range(NC)]
    far = sorted(range(NZ), key=lambda d: -min(d, NZ - d))
    return [(ys[a], zs[d], cs[b]) for d in far for a in range(NY) for b in range(NC) if a or d or b]


def by_depth(y, z, c):
    return (y * NC + c) * NZ + z


def post(source, target, sent, landed, device):
    pltpu.make_async_remote_copy(source, target, sent, landed, device_id=device, device_id_type=MESH).start()


def await_all(buffer, count, sent, landed):
    piece = buffer.at[pl.ds(0, count)]
    pltpu.make_async_copy(piece, piece, sent).wait()
    pltpu.make_async_copy(piece, piece, landed).wait()


def census_kernel(count_ref, all_ref, land_ref, sems):
    y, z, c, q = (lax.axis_index(a) for a in ("y", "z", "core", "cand"))
    here = (y * NZ + z) * NC + c
    peers = plane_peers(y, z, c)
    barrier = pltpu.get_barrier_semaphore()
    for peer in peers:
        pl.semaphore_signal(barrier, 1, device_id=peer + (q,), device_id_type=MESH)
    pl.semaphore_wait(barrier, len(peers))
    for peer in peers:
        post(count_ref, land_ref.at[here], sems.at[0], sems.at[1], peer + (q,))
    land_ref[here] = count_ref[...]
    await_all(land_ref, len(peers), sems.at[0], sems.at[1])
    all_ref[...] = land_ref[...]


def census(counts, collective_id):
    lanes = 128
    vmem = pl.BlockSpec(memory_space=pltpu.VMEM)
    shape = (NDP, 1, lanes)
    every = pl.pallas_call(
        census_kernel,
        in_specs=[vmem],
        out_specs=vmem,
        out_shape=jax.ShapeDtypeStruct(shape, counts.dtype),
        scratch_shapes=[pltpu.VMEM(shape, counts.dtype), pltpu.SemaphoreType.DMA((2,))],
        compiler_params=pltpu.CompilerParams(
            collective_id=collective_id, has_side_effects=True, vmem_limit_bytes=16 * 2**20
        ),
    )(jnp.pad(counts, (0, lanes - counts.size))[None])
    return every[:, 0, : counts.size]


def exchange_kernel(
    first_ref, second_ref, pick_ref, begin_ref, low_ref, high_ref, part_ref, got_ref, log_ref,
    back_ref, half_ref, quarters_ref, own_ref, send_ref, land_ref, sems,
):
    y, z, c, q = (lax.axis_index(a) for a in ("y", "z", "core", "cand"))
    listed = own_ref.shape[0]
    peers = plane_peers(y, z, c)
    here = by_depth(y, z, c)
    mates = [(y, z, c, lax.rem(q + d, NQ)) for d in range(1, NQ)]
    barrier = pltpu.get_barrier_semaphore()
    for peer in peers:
        pl.semaphore_signal(barrier, 1, device_id=peer + (q,), device_id_type=MESH)
    for mate in mates:
        pl.semaphore_signal(barrier, 1, device_id=mate, device_id_type=MESH)
    pl.semaphore_wait(barrier, len(peers) + len(mates))

    def send(source, target, kind, device):
        post(source, target, sems.at[kind, 0], sems.at[kind, 1], device)

    def settle(buffer, count, kind):
        await_all(buffer, count, sems.at[kind, 0], sems.at[kind, 1])

    for peer in peers:
        send(part_ref.at[by_depth(*peer)], back_ref.at[here], 0, peer + (q,))
    back_ref[here] = part_ref[here]
    settle(back_ref, len(peers), 0)

    for e in range(listed):
        half_ref[e] = joint(back_ref[first_ref[e]], back_ref[second_ref[e]])
    for n, mate in enumerate(mates):
        send(half_ref, quarters_ref.at[n], 1, mate)
    settle(quarters_ref, len(mates), 1)
    for e in range(listed):
        both = joint(half_ref[e], quarters_ref[0, e])
        rest = joint(quarters_ref[1, e], quarters_ref[2, e])
        pair = joint(both, rest)
        own_ref[e] = pair[0:1] + jnp.log(pair[1:2])

    for peer in peers:
        index = by_depth(*peer)
        send_ref[index] = own_ref[pick_ref[index]]
        send(send_ref.at[index], land_ref.at[here], 2, peer + (q,))
    land_ref[here] = own_ref[pick_ref[here]]

    grain = lax.broadcasted_iota(jnp.int32, (log_ref.shape[0], SPAN * GRAIN), 0)
    row = lax.broadcasted_iota(jnp.int32, (log_ref.shape[0], SPAN * GRAIN), 1)
    spread = jnp.zeros(grain.shape, jnp.float32)
    for e in range(listed):
        keep = (row >= low_ref[e]) & (row < high_ref[e]) & (grain - begin_ref[e] == row // GRAIN)
        spread += jnp.where(keep, own_ref[e], 0.0)
    row = lax.broadcasted_iota(jnp.int32, (SPAN * GRAIN, GRAIN), 0)
    column = lax.broadcasted_iota(jnp.int32, (SPAN * GRAIN, GRAIN), 1)
    fold = (row % GRAIN == column).astype(jnp.float32)
    log_ref[...] = jnp.dot(spread, fold, precision=lax.Precision.HIGHEST, preferred_element_type=jnp.float32)

    settle(land_ref, len(peers), 2)
    got_ref[...] = land_ref[...]


def exchange(first, second, pick, begin, low, high, part, grains, collective_id):
    listed = first.shape[0]
    span = SPAN * GRAIN
    smem, vmem = pl.BlockSpec(memory_space=pltpu.SMEM), pl.BlockSpec(memory_space=pltpu.VMEM)
    buffer = lambda *shape: pltpu.VMEM(shape + (span,), jnp.float32)
    return pl.pallas_call(
        exchange_kernel,
        in_specs=[smem] * 6 + [vmem],
        out_specs=[vmem, vmem],
        out_shape=[
            jax.ShapeDtypeStruct((NDP, 1, span), jnp.float32),
            jax.ShapeDtypeStruct((grains, GRAIN), jnp.float32),
        ],
        scratch_shapes=[
            buffer(NDP, 2), buffer(listed, 2), buffer(NQ - 1, listed, 2), buffer(listed, 1), buffer(NDP, 1), buffer(NDP, 1),
            pltpu.SemaphoreType.DMA((3, 2)),
        ],
        compiler_params=pltpu.CompilerParams(
            collective_id=collective_id, has_side_effects=True, vmem_limit_bytes=16 * 2**20
        ),
    )(first, second, pick, begin, low, high, part)


def on_device(embeddings, point_parent, parent_list, block_slots, centroids):
    y, z, c, q = (lax.axis_index(a) for a in ("y", "z", "core", "cand"))
    here = (y * NZ + z) * NC + c
    row_count, width = embeddings.shape
    stored = centroids.shape[0]
    listed = parent_list.shape[1]
    grains = row_count // GRAIN
    local = grains // NQ
    i32 = jnp.int32

    share = lax.dynamic_index_in_dim(embeddings.reshape(local, NQ, GRAIN, width), q, 1, keepdims=False)
    shares = lax.all_gather(share, ("z", "core"), axis=0, tiled=True)

    counts = jnp.sum((point_parent[:, None] == parent_list[here][None, :]).astype(i32), axis=0)
    counts = census(counts, 2)
    starts = jnp.cumsum(counts, axis=1) - counts
    begin = starts // GRAIN
    last = (starts + counts - 1) // GRAIN
    low = starts % GRAIN
    high = low + counts
    slots = jnp.take(block_slots, parent_list, axis=0)
    owner = slots // (stored * NQ)
    planes = jnp.arange(NQ, dtype=i32)

    def share_of(begin, last, plane):
        nearest = begin + (plane - begin) % NQ
        return nearest, (nearest <= last).astype(i32) + (nearest + NQ <= last).astype(i32)

    loads = share_of(begin[..., None], last[..., None], planes)[1]
    loads = jnp.broadcast_to(loads[:, :, None, :], (NDP, listed, 2, NQ)).reshape(NY, PER_Y * listed * 2, NQ)
    takers = jnp.swapaxes(owner, 2, 3).reshape(NY, PER_Y * listed * 2, NQ)
    takes = takers[..., None] == jnp.arange(NDP, dtype=i32)
    totals = jnp.einsum(
        "ymqj,ymp->yqjp", takes.astype(jnp.bfloat16), loads.astype(jnp.bfloat16), preferred_element_type=jnp.float32
    )
    size = jnp.sum((jnp.max(totals) > jnp.asarray(ROOMS[:-1], jnp.float32)).astype(i32))
    room = jnp.asarray(ROOMS, i32)[size][None]

    mine = jnp.take(owner, q, axis=2) == here
    entry = jnp.any(mine, axis=2)
    chosen = lambda value: jnp.sum(jnp.where(entry, value, 0), axis=1)
    served = jnp.any(entry, axis=1)
    serve_low, serve_high, serve_begin = chosen(low), chosen(high), chosen(begin)
    serve_last = jnp.where(served, chosen(last), -1)
    serve_block = jnp.sum(jnp.where(mine, jnp.take(slots, q, axis=2) % stored, 0), axis=(1, 2))
    grouped = served.reshape(NY, PER_Y).astype(i32)
    many = jnp.sum(grouped, axis=1)
    rank = jnp.where(
        grouped > 0, jnp.cumsum(grouped, axis=1) - 1, many[:, None] + jnp.cumsum(1 - grouped, axis=1) - 1
    )
    around = jnp.arange(PER_Y, dtype=i32)
    order = jnp.sum(jnp.where(rank[:, :, None] == around, around[None, :, None], 0), axis=1).reshape(-1)
    serving = (serve_block, serve_low, serve_high, order, many)

    _, landing = share_of(serve_begin[:, None], serve_last[:, None], planes)
    landing = landing.reshape(NY, PER_Y, NQ)
    base = (jnp.cumsum(landing, axis=1) - landing).reshape(NDP, NQ)
    step = jnp.arange(SPAN, dtype=i32)
    grain = serve_begin[:, None] + step
    plane = grain % NQ
    within = jnp.sum(jnp.where(plane[..., None] == planes, base[:, None, :], 0), axis=2) + step // NQ
    real = grain <= serve_last[:, None]
    within = jnp.where(real, within, within[:, :1])
    plane = jnp.where(real, plane, plane[:, :1])
    within = jnp.where(served[:, None], within, 0)

    own = lambda value: lax.dynamic_index_in_dim(value, here, 0, keepdims=False)
    dps = jnp.arange(NDP, dtype=i32)
    depth_order = dps.reshape(NY, NZ, NC).transpose(0, 2, 1).reshape(-1)
    own_owner = own(jnp.take(owner, q, axis=2))
    pick = jnp.sum(
        jnp.where(own_owner[None] == depth_order[:, None, None], jnp.arange(listed, dtype=i32)[None, :, None], 0),
        axis=(1, 2),
    )
    deep = lambda index: by_depth(index // PER_Y, index // NC % NZ, index % NC)

    of_y = lambda value: lax.dynamic_index_in_dim(value.reshape((NY, PER_Y) + value.shape[1:]), y, 0, keepdims=False)
    target = (jnp.arange(NY, dtype=i32) * NZ + z) * NC + c
    hit = jnp.any(of_y(owner)[None] == target[:, None, None, None, None], axis=-1)
    sent = lambda value: jnp.sum(jnp.where(hit, of_y(value)[None, :, :, None], 0), axis=2)
    nearest, sending = share_of(sent(begin), jnp.where(jnp.any(hit, axis=2), sent(last), -1), q)
    place = jnp.cumsum(sending, axis=1) - sending
    places = jnp.arange(FULL, dtype=i32)
    picks = 0
    for slot in range(2):
        here_now = (place[..., None] + slot == places) & (sending[..., None] > slot)
        which = around[:, None] * local + nearest // NQ + slot
        picks = picks + jnp.sum(jnp.where(here_now, which[..., None], 0), axis=1)
    picks = picks.reshape(NY * NQ, FULL)

    branches = [functools.partial(dispatch, most, 3 + n) for n, most in enumerate(ROOMS)]
    rows = lax.switch(size, branches, shares, picks)
    rows = rows.reshape(NY, NQ, FULL, GRAIN, width)
    spots = plane * FULL + within
    logits, part = score(rows, spots, serving, room, centroids)
    norms, log_norms = exchange(
        deep(own_owner[:, 0]), deep(own_owner[:, 1]), pick, own(begin), own(low), own(high), part, grains, 1
    )
    updated = update(rows, spots, serving, room, centroids, logits, norms)
    return updated, log_norms.reshape(row_count)


def solution(mesh):
    split = Mesh(mesh.devices.reshape(NY, NZ, NC, NQ), ("y", "z", "core", "cand"))
    dp = ("y", "z", "core")
    every = dp + ("cand",)
    return jax.shard_map(
        on_device,
        mesh=split,
        in_specs=(P(dp, None), P(dp), P(), P(), P(every, None, None)),
        out_specs=(P(every, None, None), P(dp)),
        check_vma=False,
    )
```

```python
import functools

import jax
import jax.numpy as jnp
from jax import lax
from jax.experimental import pallas as pl
from jax.experimental.pallas import tpu as pltpu
from jax.sharding import Mesh
from jax.sharding import PartitionSpec as P

sharpness = 3.0
prior_mass = 1.0

GRAIN = 16
SPAN = 8
NY, NZ, NC, NQ = 4, 8, 2, 4
NDP = NY * NZ * NC
PER_Y = NZ * NC
ABREAST = 4
FULL = 2 * PER_Y
ROOMS = (17, 19, 22, FULL)
STEPS = (
    ((1, 1), (3, 3), (1, 3), (3, 1), (1, 0), (3, 0), (1, 2), (3, 2)),
    ((0, 1), (0, 3), (2, 1), (2, 3), (2, 2), (0, 2), (2, 0)),
)
MESH = pl.DeviceIdType.MESH
VMEM_LIMIT = 56 * 2**20


def by_core(i):
    return (i % NC) * NZ + i // NC


def fetch(room, rows_ref, held_ref, sems, group):
    places = pl.ds(0, room)
    return pltpu.make_async_copy(rows_ref.at[group, :, places], held_ref.at[group], sems.at[group])


def window_rows(held_ref, spot_ref, group, window):
    spots = [spot_ref[window * SPAN + k] for k in range(SPAN)]
    return jnp.concatenate([held_ref[group, spot // FULL, spot % FULL] for spot in spots], axis=0)


def update_kernel(
    room, spot_ref, block_ref, low_ref, high_ref, order_ref, many_ref,
    rows_ref, cent_ref, logit_ref, norm_ref, out_ref,
    held_ref, kept_ref, sum_ref, mass_ref, done_ref, in_sem, kept_sem, out_sem,
):
    def kept(group):
        windows = pl.ds(group * PER_Y, PER_Y)
        return pltpu.make_async_copy(logit_ref.at[windows], kept_ref.at[windows], kept_sem.at[group])

    for group in range(NY):
        fetch(room, rows_ref, held_ref, in_sem, group).start()
        kept(group).start()

    sum_ref[...] = jnp.zeros_like(sum_ref)
    mass_ref[...] = jnp.zeros_like(mass_ref)

    @pl.loop(0, NY)
    def _(group):
        fetch(room, rows_ref, held_ref, in_sem, group).wait()
        kept(group).wait()

        @pl.loop(0, (many_ref[group] + ABREAST - 1) // ABREAST)
        def _(step):
            results = []
            for n in range(ABREAST):
                i = order_ref[group * PER_Y + step * ABREAST + n]
                window = group * PER_Y + i
                rows = window_rows(held_ref, spot_ref, group, window)
                place = lax.broadcasted_iota(jnp.int32, kept_ref.shape[1:], 1)
                keep = (place >= low_ref[window]) & (place < high_ref[window])
                norm = norm_ref[group * PER_Y + by_core(i)]
                weights = jnp.where(keep, jnp.exp(kept_ref[window] - norm), 0.0).astype(jnp.bfloat16)
                sums = lax.dot_general(weights, rows, (((1,), (0,)), ((), ())), preferred_element_type=jnp.float32)
                mass = jnp.sum(weights.astype(jnp.float32), axis=1, keepdims=True)
                results.append((block_ref[window], sums, mass))
            for b, sums, mass in results:
                sum_ref[b] += sums
                mass_ref[b] += mass

    def out(b):
        return pltpu.make_async_copy(done_ref.at[b], out_ref.at[b], out_sem.at[b])

    stored = cent_ref.shape[0]

    @pl.loop(0, stored)
    def _(b):
        new = (sum_ref[b] + prior_mass * cent_ref[b].astype(jnp.float32)) / (mass_ref[b] + prior_mass)
        done_ref[b] = new.astype(done_ref.dtype)
        out(b).start()
    @pl.loop(0, stored)
    def _(b):
        out(b).wait()


def update(rows, spots, serving, room, centroids, logits, norms):
    stored, lanes, width = centroids.shape
    span = SPAN * GRAIN
    smem, vmem = pl.BlockSpec(memory_space=pltpu.SMEM), pl.BlockSpec(memory_space=pltpu.VMEM)
    hbm = pl.BlockSpec(memory_space=pl.ANY)
    return pl.pallas_call(
        functools.partial(update_kernel, room),
        in_specs=[smem] * 6 + [hbm, vmem, hbm, vmem],
        out_specs=hbm,
        out_shape=jax.ShapeDtypeStruct(centroids.shape, centroids.dtype),
        scratch_shapes=[
            pltpu.VMEM((NY, NQ, room) + rows.shape[3:], rows.dtype),
            pltpu.VMEM((NDP, lanes, span), jnp.float32),
            pltpu.VMEM((stored, lanes, width), jnp.float32),
            pltpu.VMEM((stored, lanes, 1), jnp.float32),
            pltpu.VMEM(centroids.shape, centroids.dtype),
            pltpu.SemaphoreType.DMA((NY,)),
            pltpu.SemaphoreType.DMA((NY,)),
            pltpu.SemaphoreType.DMA((stored,)),
        ],
        compiler_params=pltpu.CompilerParams(vmem_limit_bytes=VMEM_LIMIT),
        cost_estimate=pl.CostEstimate(
            flops=NDP * lanes * span * width, bytes_accessed=2 * rows.size, transcendentals=NDP * lanes * span
        ),
    )(spots, *serving, rows, centroids, logits, norms)


def joint(former, latter):
    highest = jnp.maximum(former[0:1], latter[0:1])
    total = former[1:2] * jnp.exp(former[0:1] - highest) + latter[1:2] * jnp.exp(latter[0:1] - highest)
    return jnp.concatenate([highest, total], axis=0)


def plane_peers(y, z, c):
    ys = [lax.rem(y + d, NY) for d in range(NY)]
    zs = [lax.rem(z + d, NZ) for d in range(NZ)]
    cs = [lax.rem(c + d, NC) for d in range(NC)]
    far = sorted(range(NZ), key=lambda d: -min(d, NZ - d))
    return [(ys[a], zs[d], cs[b]) for d in far for a in range(NY) for b in range(NC) if a or d or b]


def by_depth(y, z, c):
    return (y * NC + c) * NZ + z


def post(source, target, sent, landed, device):
    pltpu.make_async_remote_copy(source, target, sent, landed, device_id=device, device_id_type=MESH).start()


def await_all(buffer, count, sent, landed):
    piece = buffer.at[pl.ds(0, count)]
    pltpu.make_async_copy(piece, piece, sent).wait()
    pltpu.make_async_copy(piece, piece, landed).wait()


def census_kernel(count_ref, all_ref, land_ref, sems):
    y, z, c, q = (lax.axis_index(a) for a in ("y", "z", "core", "cand"))
    here = (y * NZ + z) * NC + c
    peers = plane_peers(y, z, c)
    barrier = pltpu.get_barrier_semaphore()
    for peer in peers:
        pl.semaphore_signal(barrier, 1, device_id=peer + (q,), device_id_type=MESH)
    pl.semaphore_wait(barrier, len(peers))
    for peer in peers:
        post(count_ref, land_ref.at[here], sems.at[0], sems.at[1], peer + (q,))
    land_ref[here] = count_ref[...]
    await_all(land_ref, len(peers), sems.at[0], sems.at[1])
    all_ref[...] = land_ref[...]


def census(counts, collective_id):
    lanes = 128
    vmem = pl.BlockSpec(memory_space=pltpu.VMEM)
    shape = (NDP, 1, lanes)
    every = pl.pallas_call(
        census_kernel,
        in_specs=[vmem],
        out_specs=vmem,
        out_shape=jax.ShapeDtypeStruct(shape, counts.dtype),
        scratch_shapes=[pltpu.VMEM(shape, counts.dtype), pltpu.SemaphoreType.DMA((2,))],
        compiler_params=pltpu.CompilerParams(
            collective_id=collective_id, has_side_effects=True, vmem_limit_bytes=16 * 2**20
        ),
    )(jnp.pad(counts, (0, lanes - counts.size))[None])
    return every[:, 0, : counts.size]


def serve_kernel(
    room, pick_ref, spot_ref, block_ref, first_ref, second_ref, entry_ref, begin_ref, low_ref, high_ref,
    share_ref, cent_ref, rows_ref, logit_ref, got_ref, log_ref,
    grains_ref, send_ref, held_refs, kept_ref, square_ref, part_ref,
    back_ref, half_ref, quarters_ref, own_ref, fore_ref, land_ref,
    load_sem, send_sem, recv_sem, out_sem, sems,
):
    y, z, c, q = (lax.axis_index(a) for a in ("y", "z", "core", "cand"))
    here = y * NQ + q
    deep = by_depth(y, z, c)
    peers = plane_peers(y, z, c)
    mates = [(y, z, c, lax.rem(q + d, NQ)) for d in range(1, NQ)]

    def target(step):
        ty, tq = lax.rem(y + step[0], NY), lax.rem(q + step[1], NQ)
        return ty * NQ + tq, (ty, z, c, tq)

    load = pltpu.make_async_copy(share_ref, grains_ref, load_sem.at[0])
    load.start()
    slanted = [target(step)[1] for phase in STEPS for step in phase if step[0] and step[1]]
    barrier = pltpu.get_barrier_semaphore()
    for device in [peer + (q,) for peer in peers] + mates + slanted:
        pl.semaphore_signal(barrier, 1, device_id=device, device_id_type=MESH)
    pl.semaphore_wait(barrier, len(peers) + len(mates) + len(slanted))
    load.wait()

    def lands(phase, step):
        return held_refs[phase].at[((NY - step[0]) % NY) // 2 * NQ + q]

    def copy(phase, n, places):
        step = STEPS[phase][n]
        index, device = target(step)
        return pltpu.make_async_remote_copy(
            send_ref.at[index, places], lands(phase, step).at[places], send_sem.at[phase, n], recv_sem.at[phase, n],
            device_id=device, device_id_type=MESH,
        )

    for phase, steps in enumerate(STEPS):

        @pl.loop(0, room)
        def _(place):
            for n, step in enumerate(steps):
                index, _ = target(step)
                send_ref[index, place] = grains_ref[pick_ref[index * FULL + place]]
                copy(phase, n, pl.ds(place, 1)).start()
            if phase == 1:
                send_ref[here, place] = grains_ref[pick_ref[here * FULL + place]]

    kept = pltpu.make_async_copy(send_ref.at[here], lands(1, (0, 0)), load_sem.at[1])
    kept.start()

    @pl.loop(0, cent_ref.shape[0])
    def _(b):
        wide = cent_ref[b].astype(jnp.float32)
        square_ref[b] = jnp.sum(wide * wide, axis=1, keepdims=True)

    def group_of(phase, side):
        return lax.rem(y + 2 * side + 1 - phase, NY)

    def rows_out(phase, side):
        return pltpu.make_async_copy(
            held_refs[phase].at[pl.ds(side * NQ, NQ)],
            rows_ref.at[pl.ds(group_of(phase, side) * NQ, NQ), pl.ds(0, room)],
            out_sem.at[phase, side, 0],
        )

    def logits_out(phase, side):
        windows = pl.ds(group_of(phase, side) * PER_Y, PER_Y)
        return pltpu.make_async_copy(kept_ref.at[windows], logit_ref.at[windows], out_sem.at[phase, side, 1])

    for phase, steps in enumerate(STEPS):
        held_ref = held_refs[phase]
        for n in range(len(steps)):
            copy(phase, n, pl.ds(0, room)).wait()
        if phase == 1:
            kept.wait()
        turns = PER_Y // ABREAST

        for side in range(2):
            rows_out(phase, side).start()

        @pl.loop(0, 2 * turns)
        def _(turn):
            side = turn // turns
            group = group_of(phase, side)
            places = [turn % turns * ABREAST + n for n in range(ABREAST)]
            results = []
            for i in places:
                window = group * PER_Y + i
                spots = [spot_ref[window * SPAN + k] for k in range(SPAN)]
                rows = jnp.concatenate([held_ref[side * NQ + spot // FULL, spot % FULL] for spot in spots], axis=0)
                b = block_ref[window]
                scores = lax.dot_general(
                    cent_ref[b], rows, (((1,), (1,)), ((), ())), preferred_element_type=jnp.float32
                )
                logits = sharpness * (scores - 0.5 * square_ref[b])
                highest = jnp.max(logits, axis=0, keepdims=True)
                total = jnp.sum(jnp.exp(logits - highest), axis=0, keepdims=True)
                results.append((logits, jnp.concatenate([highest, total], axis=0)))
            for i, (logits, part) in zip(places, results):
                kept_ref[group * PER_Y + i] = logits
                part_ref[group * PER_Y + by_core(i)] = part

        for side in range(2):
            logits_out(phase, side).start()

    def settle(buffer, count, kind):
        await_all(buffer, count, sems.at[kind, 0], sems.at[kind, 1])

    for peer in peers:
        post(part_ref.at[by_depth(*peer)], back_ref.at[deep], sems.at[0, 0], sems.at[0, 1], peer + (q,))
    back_ref[deep] = part_ref[deep]
    settle(back_ref, len(peers), 0)

    listed = own_ref.shape[0]
    for e in range(listed):
        half_ref[e] = joint(back_ref[first_ref[e]], back_ref[second_ref[e]])
    for n, mate in enumerate(mates):
        post(half_ref, quarters_ref.at[n], sems.at[1, 0], sems.at[1, 1], mate)
    settle(quarters_ref, len(mates), 1)
    for e in range(listed):
        both = joint(half_ref[e], quarters_ref[0, e])
        rest = joint(quarters_ref[1, e], quarters_ref[2, e])
        pair = joint(both, rest)
        own_ref[e] = pair[0:1] + jnp.log(pair[1:2])

    for peer in peers:
        index = by_depth(*peer)
        fore_ref[index] = own_ref[entry_ref[index]]
        post(fore_ref.at[index], land_ref.at[deep], sems.at[2, 0], sems.at[2, 1], peer + (q,))
    land_ref[deep] = own_ref[entry_ref[deep]]

    grain = lax.broadcasted_iota(jnp.int32, (log_ref.shape[0], SPAN * GRAIN), 0)
    row = lax.broadcasted_iota(jnp.int32, (log_ref.shape[0], SPAN * GRAIN), 1)
    spread = jnp.zeros(grain.shape, jnp.float32)
    for e in range(listed):
        keep = (row >= low_ref[e]) & (row < high_ref[e]) & (grain - begin_ref[e] == row // GRAIN)
        spread += jnp.where(keep, own_ref[e], 0.0)
    row = lax.broadcasted_iota(jnp.int32, (SPAN * GRAIN, GRAIN), 0)
    column = lax.broadcasted_iota(jnp.int32, (SPAN * GRAIN, GRAIN), 1)
    fold = (row % GRAIN == column).astype(jnp.float32)
    log_ref[...] = jnp.dot(spread, fold, precision=lax.Precision.HIGHEST, preferred_element_type=jnp.float32)

    settle(land_ref, len(peers), 2)
    got_ref[...] = land_ref[...]
    for phase in range(2):
        for side in range(2):
            rows_out(phase, side).wait()
            logits_out(phase, side).wait()


def serve(room, collective_id, grains, shares, centroids, *tables):
    stored, lanes, width = centroids.shape
    span = SPAN * GRAIN
    targets = NY * NQ
    listed = tables[3].shape[0]
    shape, dtype = shares.shape[1:], shares.dtype
    smem, vmem = pl.BlockSpec(memory_space=pltpu.SMEM), pl.BlockSpec(memory_space=pltpu.VMEM)
    hbm = pl.BlockSpec(memory_space=pl.ANY)
    buffer = lambda *shape: pltpu.VMEM(shape + (span,), jnp.float32)
    dma = pltpu.SemaphoreType.DMA
    return pl.pallas_call(
        functools.partial(serve_kernel, room),
        in_specs=[smem] * len(tables) + [hbm, vmem],
        out_specs=[hbm, hbm, vmem, vmem],
        out_shape=[
            jax.ShapeDtypeStruct((targets, FULL) + shape, dtype),
            jax.ShapeDtypeStruct((NDP, lanes, span), jnp.float32),
            jax.ShapeDtypeStruct((NDP, 1, span), jnp.float32),
            jax.ShapeDtypeStruct((grains, GRAIN), jnp.float32),
        ],
        scratch_shapes=[
            pltpu.VMEM(shares.shape, dtype),
            pltpu.VMEM((targets, room) + shape, dtype),
            [pltpu.VMEM((targets // 2, room) + shape, dtype)] * 2,
            buffer(NDP, lanes),
            pltpu.VMEM((stored, lanes, 1), jnp.float32),
            buffer(NDP, 2),
            buffer(NDP, 2), buffer(listed, 2), buffer(NQ - 1, listed, 2), buffer(listed, 1), buffer(NDP, 1), buffer(NDP, 1),
            dma((2,)), dma((2, targets // 2)), dma((2, targets // 2)), dma((2, 2, 2)), dma((3, 2)),
        ],
        compiler_params=pltpu.CompilerParams(
            collective_id=collective_id, has_side_effects=True, vmem_limit_bytes=VMEM_LIMIT
        ),
        cost_estimate=pl.CostEstimate(
            flops=2 * NDP * lanes * span * width,
            bytes_accessed=2 * (shares.size + 3 * targets * room * shape[0] * shape[1]),
            transcendentals=NDP * lanes * span,
        ),
    )(*tables, shares, centroids)


def on_device(embeddings, point_parent, parent_list, block_slots, centroids):
    y, z, c, q = (lax.axis_index(a) for a in ("y", "z", "core", "cand"))
    here = (y * NZ + z) * NC + c
    row_count, width = embeddings.shape
    stored = centroids.shape[0]
    listed = parent_list.shape[1]
    grains = row_count // GRAIN
    local = grains // NQ
    i32 = jnp.int32

    share = lax.dynamic_index_in_dim(embeddings.reshape(local, NQ, GRAIN, width), q, 1, keepdims=False)
    shares = lax.all_gather(share, ("z", "core"), axis=0, tiled=True)

    counts = jnp.sum((point_parent[:, None] == parent_list[here][None, :]).astype(i32), axis=0)
    counts = census(counts, 1)
    starts = jnp.cumsum(counts, axis=1) - counts
    begin = starts // GRAIN
    last = (starts + counts - 1) // GRAIN
    low = starts % GRAIN
    high = low + counts
    slots = jnp.take(block_slots, parent_list, axis=0)
    owner = slots // (stored * NQ)
    planes = jnp.arange(NQ, dtype=i32)

    def share_of(begin, last, plane):
        nearest = begin + (plane - begin) % NQ
        return nearest, (nearest <= last).astype(i32) + (nearest + NQ <= last).astype(i32)

    loads = share_of(begin[..., None], last[..., None], planes)[1]
    loads = jnp.broadcast_to(loads[:, :, None, :], (NDP, listed, 2, NQ)).reshape(NY, PER_Y * listed * 2, NQ)
    takers = jnp.swapaxes(owner, 2, 3).reshape(NY, PER_Y * listed * 2, NQ)
    takes = takers[..., None] == jnp.arange(NDP, dtype=i32)
    totals = jnp.einsum(
        "ymqj,ymp->yqjp", takes.astype(jnp.bfloat16), loads.astype(jnp.bfloat16), preferred_element_type=jnp.float32
    )
    size = jnp.sum((jnp.max(totals) > jnp.asarray(ROOMS[:-1], jnp.float32)).astype(i32))

    mine = jnp.take(owner, q, axis=2) == here
    entry = jnp.any(mine, axis=2)
    chosen = lambda value: jnp.sum(jnp.where(entry, value, 0), axis=1)
    served = jnp.any(entry, axis=1)
    serve_low, serve_high, serve_begin = chosen(low), chosen(high), chosen(begin)
    serve_last = jnp.where(served, chosen(last), -1)
    serve_block = jnp.sum(jnp.where(mine, jnp.take(slots, q, axis=2) % stored, 0), axis=(1, 2))
    grouped = served.reshape(NY, PER_Y).astype(i32)
    many = jnp.sum(grouped, axis=1)
    rank = jnp.where(
        grouped > 0, jnp.cumsum(grouped, axis=1) - 1, many[:, None] + jnp.cumsum(1 - grouped, axis=1) - 1
    )
    around = jnp.arange(PER_Y, dtype=i32)
    order = jnp.sum(jnp.where(rank[:, :, None] == around, around[None, :, None], 0), axis=1).reshape(-1)
    serving = (serve_block, serve_low, serve_high, order, many)

    _, landing = share_of(serve_begin[:, None], serve_last[:, None], planes)
    landing = landing.reshape(NY, PER_Y, NQ)
    base = (jnp.cumsum(landing, axis=1) - landing).reshape(NDP, NQ)
    step = jnp.arange(SPAN, dtype=i32)
    grain = serve_begin[:, None] + step
    plane = grain % NQ
    within = jnp.sum(jnp.where(plane[..., None] == planes, base[:, None, :], 0), axis=2) + step // NQ
    real = grain <= serve_last[:, None]
    within = jnp.where(real, within, within[:, :1])
    plane = jnp.where(real, plane, plane[:, :1])
    within = jnp.where(served[:, None], within, 0)

    own = lambda value: lax.dynamic_index_in_dim(value, here, 0, keepdims=False)
    dps = jnp.arange(NDP, dtype=i32)
    depth_order = dps.reshape(NY, NZ, NC).transpose(0, 2, 1).reshape(-1)
    own_owner = own(jnp.take(owner, q, axis=2))
    pick = jnp.sum(
        jnp.where(own_owner[None] == depth_order[:, None, None], jnp.arange(listed, dtype=i32)[None, :, None], 0),
        axis=(1, 2),
    )
    deep = lambda index: by_depth(index // PER_Y, index // NC % NZ, index % NC)

    of_y = lambda value: lax.dynamic_index_in_dim(value.reshape((NY, PER_Y) + value.shape[1:]), y, 0, keepdims=False)
    target = (jnp.arange(NY, dtype=i32) * NZ + z) * NC + c
    hit = jnp.any(of_y(owner)[None] == target[:, None, None, None, None], axis=-1)
    sent = lambda value: jnp.sum(jnp.where(hit, of_y(value)[None, :, :, None], 0), axis=2)
    nearest, sending = share_of(sent(begin), jnp.where(jnp.any(hit, axis=2), sent(last), -1), q)
    place = jnp.cumsum(sending, axis=1) - sending
    places = jnp.arange(FULL, dtype=i32)
    picks = 0
    for slot in range(2):
        here_now = (place[..., None] + slot == places) & (sending[..., None] > slot)
        which = around[:, None] * local + nearest // NQ + slot
        picks = picks + jnp.sum(jnp.where(here_now, which[..., None], 0), axis=1)

    tables = (picks.reshape(-1), (plane * FULL + within).reshape(-1), serve_block)
    tables += (deep(own_owner[:, 0]), deep(own_owner[:, 1]), pick, own(begin), own(low), own(high))
    tables = lax.optimization_barrier(tables)

    def finish(most, collective_id, shares, centroids, *tables):
        rows, logits, norms, log_norms = serve(most, collective_id, grains, shares, centroids, *tables)
        rows = rows.reshape(NY, NQ, FULL, GRAIN, width)
        return update(rows, tables[1], serving, most, centroids, logits, norms), log_norms

    branches = [functools.partial(finish, most, 2 + n) for n, most in enumerate(ROOMS)]
    updated, log_norms = lax.switch(size, branches, shares, centroids, *tables)
    return updated, log_norms.reshape(row_count)


def solution(mesh):
    split = Mesh(mesh.devices.reshape(NY, NZ, NC, NQ), ("y", "z", "core", "cand"))
    dp = ("y", "z", "core")
    every = dp + ("cand",)
    return jax.shard_map(
        on_device,
        mesh=split,
        in_specs=(P(dp, None), P(dp), P(), P(), P(every, None, None)),
        out_specs=(P(every, None, None), P(dp)),
        check_vma=False,
    )
```

```python
import functools

import jax
import jax.numpy as jnp
from jax import lax
from jax.experimental import pallas as pl
from jax.experimental.pallas import tpu as pltpu
from jax.sharding import Mesh
from jax.sharding import PartitionSpec as P

sharpness = 3.0
prior_mass = 1.0

GRAIN = 16
SPAN = 8
NY, NZ, NC, NQ = 4, 8, 2, 4
NDP = NY * NZ * NC
PER_Y = NZ * NC
ABREAST = 4
FULL = 2 * PER_Y
ROOMS = (16, 17, 20, FULL)
SPARE = 5
STEPS = (
    ((1, 1), (3, 3), (1, 3), (3, 1), (1, 0), (3, 0), (1, 2), (3, 2)),
    ((0, 1), (0, 3), (2, 1), (2, 3), (2, 2), (0, 2), (2, 0)),
)
MESH = pl.DeviceIdType.MESH
VMEM_LIMIT = 56 * 2**20


def by_core(i):
    return (i % NC) * NZ + i // NC


def fetch(room, rows_ref, held_ref, sems, group):
    places = pl.ds(0, room)
    return pltpu.make_async_copy(rows_ref.at[group, :, places], held_ref.at[group], sems.at[group])


def window_rows(held_ref, spot_ref, group, window):
    spots = [spot_ref[window * SPAN + k] for k in range(SPAN)]
    return jnp.concatenate([held_ref[group, spot // FULL, spot % FULL] for spot in spots], axis=0)


def update_kernel(
    room, spot_ref, block_ref, low_ref, high_ref, order_ref, many_ref,
    rows_ref, cent_ref, logit_ref, norm_ref, out_ref,
    held_ref, kept_ref, sum_ref, mass_ref, done_ref, in_sem, kept_sem, out_sem,
):
    def kept(group):
        windows = pl.ds(group * PER_Y, PER_Y)
        return pltpu.make_async_copy(logit_ref.at[windows], kept_ref.at[windows], kept_sem.at[group])

    for group in range(NY):
        fetch(room, rows_ref, held_ref, in_sem, group).start()
        kept(group).start()

    sum_ref[...] = jnp.zeros_like(sum_ref)
    mass_ref[...] = jnp.zeros_like(mass_ref)

    @pl.loop(0, NY)
    def _(group):
        fetch(room, rows_ref, held_ref, in_sem, group).wait()
        kept(group).wait()

        @pl.loop(0, (many_ref[group] + ABREAST - 1) // ABREAST)
        def _(step):
            results = []
            for n in range(ABREAST):
                i = order_ref[group * PER_Y + step * ABREAST + n]
                window = group * PER_Y + i
                rows = window_rows(held_ref, spot_ref, group, window)
                place = lax.broadcasted_iota(jnp.int32, kept_ref.shape[1:], 1)
                keep = (place >= low_ref[window]) & (place < high_ref[window])
                norm = norm_ref[group * PER_Y + by_core(i)]
                weights = jnp.where(keep, jnp.exp(kept_ref[window] - norm), 0.0).astype(jnp.bfloat16)
                sums = lax.dot_general(weights, rows, (((1,), (0,)), ((), ())), preferred_element_type=jnp.float32)
                mass = jnp.sum(weights.astype(jnp.float32), axis=1, keepdims=True)
                results.append((block_ref[window], sums, mass))
            for b, sums, mass in results:
                sum_ref[b] += sums
                mass_ref[b] += mass

    def out(b):
        return pltpu.make_async_copy(done_ref.at[b], out_ref.at[b], out_sem.at[b])

    stored = cent_ref.shape[0]

    @pl.loop(0, stored)
    def _(b):
        new = (sum_ref[b] + prior_mass * cent_ref[b].astype(jnp.float32)) / (mass_ref[b] + prior_mass)
        done_ref[b] = new.astype(done_ref.dtype)
        out(b).start()
    @pl.loop(0, stored)
    def _(b):
        out(b).wait()


def update(rows, spots, serving, room, centroids, logits, norms):
    stored, lanes, width = centroids.shape
    span = SPAN * GRAIN
    smem, vmem = pl.BlockSpec(memory_space=pltpu.SMEM), pl.BlockSpec(memory_space=pltpu.VMEM)
    hbm = pl.BlockSpec(memory_space=pl.ANY)
    return pl.pallas_call(
        functools.partial(update_kernel, room),
        in_specs=[smem] * 6 + [hbm, vmem, hbm, vmem],
        out_specs=hbm,
        out_shape=jax.ShapeDtypeStruct(centroids.shape, centroids.dtype),
        scratch_shapes=[
            pltpu.VMEM((NY, NQ, room) + rows.shape[3:], rows.dtype),
            pltpu.VMEM((NDP, lanes, span), jnp.float32),
            pltpu.VMEM((stored, lanes, width), jnp.float32),
            pltpu.VMEM((stored, lanes, 1), jnp.float32),
            pltpu.VMEM(centroids.shape, centroids.dtype),
            pltpu.SemaphoreType.DMA((NY,)),
            pltpu.SemaphoreType.DMA((NY,)),
            pltpu.SemaphoreType.DMA((stored,)),
        ],
        compiler_params=pltpu.CompilerParams(vmem_limit_bytes=VMEM_LIMIT),
        cost_estimate=pl.CostEstimate(
            flops=NDP * lanes * span * width, bytes_accessed=2 * rows.size, transcendentals=NDP * lanes * span
        ),
    )(spots, *serving, rows, centroids, logits, norms)


def joint(former, latter):
    highest = jnp.maximum(former[0:1], latter[0:1])
    total = former[1:2] * jnp.exp(former[0:1] - highest) + latter[1:2] * jnp.exp(latter[0:1] - highest)
    return jnp.concatenate([highest, total], axis=0)


def plane_peers(y, z, c):
    ys = [lax.rem(y + d, NY) for d in range(NY)]
    zs = [lax.rem(z + d, NZ) for d in range(NZ)]
    cs = [lax.rem(c + d, NC) for d in range(NC)]
    far = sorted(range(NZ), key=lambda d: -min(d, NZ - d))
    return [(ys[a], zs[d], cs[b]) for d in far for a in range(NY) for b in range(NC) if a or d or b]


def by_depth(y, z, c):
    return (y * NC + c) * NZ + z


def post(source, target, sent, landed, device):
    pltpu.make_async_remote_copy(source, target, sent, landed, device_id=device, device_id_type=MESH).start()


def await_all(buffer, count, sent, landed):
    piece = buffer.at[pl.ds(0, count)]
    pltpu.make_async_copy(piece, piece, sent).wait()
    pltpu.make_async_copy(piece, piece, landed).wait()


def census_kernel(count_ref, all_ref, land_ref, sems):
    y, z, c, q = (lax.axis_index(a) for a in ("y", "z", "core", "cand"))
    here = (y * NZ + z) * NC + c
    peers = plane_peers(y, z, c)
    barrier = pltpu.get_barrier_semaphore()
    for peer in peers:
        pl.semaphore_signal(barrier, 1, device_id=peer + (q,), device_id_type=MESH)
    pl.semaphore_wait(barrier, len(peers))
    for peer in peers:
        post(count_ref, land_ref.at[here], sems.at[0], sems.at[1], peer + (q,))
    land_ref[here] = count_ref[...]
    await_all(land_ref, len(peers), sems.at[0], sems.at[1])
    all_ref[...] = land_ref[...]


def census(counts, collective_id):
    lanes = 128
    vmem = pl.BlockSpec(memory_space=pltpu.VMEM)
    shape = (NDP, 1, lanes)
    every = pl.pallas_call(
        census_kernel,
        in_specs=[vmem],
        out_specs=vmem,
        out_shape=jax.ShapeDtypeStruct(shape, counts.dtype),
        scratch_shapes=[pltpu.VMEM(shape, counts.dtype), pltpu.SemaphoreType.DMA((2,))],
        compiler_params=pltpu.CompilerParams(
            collective_id=collective_id, has_side_effects=True, vmem_limit_bytes=16 * 2**20
        ),
    )(jnp.pad(counts, (0, lanes - counts.size))[None])
    return every[:, 0, : counts.size]


def serve_kernel(
    room, pick_ref, spot_ref, block_ref, first_ref, second_ref, entry_ref, begin_ref, low_ref, high_ref,
    share_ref, cent_ref, rows_ref, logit_ref, got_ref, log_ref,
    grains_ref, send_ref, held_refs, kept_ref, square_ref, part_ref,
    back_ref, half_ref, quarters_ref, own_ref, fore_ref, land_ref,
    load_sem, send_sem, recv_sem, hand_sem, out_sem, sems,
):
    y, z, c, q = (lax.axis_index(a) for a in ("y", "z", "core", "cand"))
    here = y * NQ + q
    deep = by_depth(y, z, c)
    spare = min(SPARE, FULL - room)
    front, back = pl.ds(0, room - spare), pl.ds(room - spare, spare)
    peers = plane_peers(y, z, c)
    mates = [(y, z, c, lax.rem(q + d, NQ)) for d in range(1, NQ)]

    def target(step):
        ty, tq = lax.rem(y + step[0], NY), lax.rem(q + step[1], NQ)
        return ty * NQ + tq, (ty, z, c, tq)

    load = pltpu.make_async_copy(share_ref, grains_ref, load_sem.at[0])
    load.start()
    slanted = [target(step)[1] for phase in STEPS for step in phase if step[0] and step[1]]
    barrier = pltpu.get_barrier_semaphore()
    for device in [peer + (q,) for peer in peers] + mates + slanted:
        pl.semaphore_signal(barrier, 1, device_id=device, device_id_type=MESH)
    pl.semaphore_wait(barrier, len(peers) + len(mates) + len(slanted))
    load.wait()

    def lands(phase, step):
        return held_refs[phase].at[((NY - step[0]) % NY) // 2 * NQ + q]

    def copy(phase, n, places, part):
        step = STEPS[phase][n]
        index, device = target(step)
        return pltpu.make_async_remote_copy(
            send_ref.at[index, places], lands(phase, step).at[places],
            send_sem.at[phase, part, n], recv_sem.at[phase, part, n], device_id=device, device_id_type=MESH,
        )

    for phase, steps in enumerate(STEPS):

        @pl.loop(0, room)
        def _(turn):
            place, part = (turn + room - spare) % room, (turn + room - spare) // room
            for n, step in enumerate(steps):
                index, _ = target(step)
                send_ref[index, place] = grains_ref[pick_ref[index * FULL + place]]
                copy(phase, n, pl.ds(place, 1), part).start()
            if phase == 1:
                send_ref[here, place] = grains_ref[pick_ref[here * FULL + place]]

    kept = pltpu.make_async_copy(send_ref.at[here], lands(1, (0, 0)).at[pl.ds(0, room)], load_sem.at[1])
    kept.start()

    def hand(phase):
        held_ref = held_refs[phase]
        return pltpu.make_async_remote_copy(
            held_ref.at[:, back], held_ref.at[:, pl.ds(room, spare)], hand_sem.at[phase, 0], hand_sem.at[phase, 1],
            device_id=(y, z, 1 - c, q), device_id_type=MESH,
        )

    @pl.loop(0, cent_ref.shape[0])
    def _(b):
        wide = cent_ref[b].astype(jnp.float32)
        square_ref[b] = jnp.sum(wide * wide, axis=1, keepdims=True)

    def group_of(phase, side):
        return lax.rem(y + 2 * side + 1 - phase, NY)

    def rows_out(phase, side):
        return pltpu.make_async_copy(
            held_refs[phase].at[pl.ds(side * NQ, NQ)],
            rows_ref.at[pl.ds(group_of(phase, side) * NQ, NQ), pl.ds(0, room + spare)],
            out_sem.at[phase, side, 0],
        )

    def logits_out(phase, side):
        windows = pl.ds(group_of(phase, side) * PER_Y, PER_Y)
        return pltpu.make_async_copy(kept_ref.at[windows], logit_ref.at[windows], out_sem.at[phase, side, 1])

    for phase, steps in enumerate(STEPS):
        held_ref = held_refs[phase]
        if phase == 1:
            kept.wait()
        if spare:
            for n in range(len(steps)):
                copy(phase, n, back, 0).wait()
            hand(phase).start()
        for n in range(len(steps)):
            copy(phase, n, front, 1).wait()
        if spare:
            hand(phase).wait()
        turns = PER_Y // ABREAST

        for side in range(2):
            rows_out(phase, side).start()

        @pl.loop(0, 2 * turns)
        def _(turn):
            side = turn // turns
            group = group_of(phase, side)
            places = [turn % turns * ABREAST + n for n in range(ABREAST)]
            results = []
            for i in places:
                window = group * PER_Y + i
                spots = [spot_ref[window * SPAN + k] for k in range(SPAN)]
                rows = jnp.concatenate([held_ref[side * NQ + spot // FULL, spot % FULL] for spot in spots], axis=0)
                b = block_ref[window]
                scores = lax.dot_general(
                    cent_ref[b], rows, (((1,), (1,)), ((), ())), preferred_element_type=jnp.float32
                )
                logits = sharpness * (scores - 0.5 * square_ref[b])
                highest = jnp.max(logits, axis=0, keepdims=True)
                total = jnp.sum(jnp.exp(logits - highest), axis=0, keepdims=True)
                results.append((logits, jnp.concatenate([highest, total], axis=0)))
            for i, (logits, part) in zip(places, results):
                kept_ref[group * PER_Y + i] = logits
                part_ref[group * PER_Y + by_core(i)] = part

        for side in range(2):
            logits_out(phase, side).start()

    def settle(buffer, count, kind):
        await_all(buffer, count, sems.at[kind, 0], sems.at[kind, 1])

    for peer in peers:
        post(part_ref.at[by_depth(*peer)], back_ref.at[deep], sems.at[0, 0], sems.at[0, 1], peer + (q,))
    back_ref[deep] = part_ref[deep]
    settle(back_ref, len(peers), 0)

    listed = own_ref.shape[0]
    for e in range(listed):
        half_ref[e] = joint(back_ref[first_ref[e]], back_ref[second_ref[e]])
    for n, mate in enumerate(mates):
        post(half_ref, quarters_ref.at[n], sems.at[1, 0], sems.at[1, 1], mate)
    settle(quarters_ref, len(mates), 1)
    for e in range(listed):
        both = joint(half_ref[e], quarters_ref[0, e])
        rest = joint(quarters_ref[1, e], quarters_ref[2, e])
        pair = joint(both, rest)
        own_ref[e] = pair[0:1] + jnp.log(pair[1:2])

    for peer in peers:
        index = by_depth(*peer)
        fore_ref[index] = own_ref[entry_ref[index]]
        post(fore_ref.at[index], land_ref.at[deep], sems.at[2, 0], sems.at[2, 1], peer + (q,))
    land_ref[deep] = own_ref[entry_ref[deep]]

    grain = lax.broadcasted_iota(jnp.int32, (log_ref.shape[0], SPAN * GRAIN), 0)
    row = lax.broadcasted_iota(jnp.int32, (log_ref.shape[0], SPAN * GRAIN), 1)
    spread = jnp.zeros(grain.shape, jnp.float32)
    for e in range(listed):
        keep = (row >= low_ref[e]) & (row < high_ref[e]) & (grain - begin_ref[e] == row // GRAIN)
        spread += jnp.where(keep, own_ref[e], 0.0)
    row = lax.broadcasted_iota(jnp.int32, (SPAN * GRAIN, GRAIN), 0)
    column = lax.broadcasted_iota(jnp.int32, (SPAN * GRAIN, GRAIN), 1)
    fold = (row % GRAIN == column).astype(jnp.float32)
    log_ref[...] = jnp.dot(spread, fold, precision=lax.Precision.HIGHEST, preferred_element_type=jnp.float32)

    settle(land_ref, len(peers), 2)
    got_ref[...] = land_ref[...]
    for phase in range(2):
        for side in range(2):
            rows_out(phase, side).wait()
            logits_out(phase, side).wait()


def serve(room, collective_id, grains, shares, centroids, *tables):
    stored, lanes, width = centroids.shape
    span = SPAN * GRAIN
    targets = NY * NQ
    listed = tables[3].shape[0]
    shape, dtype = shares.shape[1:], shares.dtype
    smem, vmem = pl.BlockSpec(memory_space=pltpu.SMEM), pl.BlockSpec(memory_space=pltpu.VMEM)
    hbm = pl.BlockSpec(memory_space=pl.ANY)
    buffer = lambda *shape: pltpu.VMEM(shape + (span,), jnp.float32)
    dma = pltpu.SemaphoreType.DMA
    return pl.pallas_call(
        functools.partial(serve_kernel, room),
        in_specs=[smem] * len(tables) + [hbm, vmem],
        out_specs=[hbm, hbm, vmem, vmem],
        out_shape=[
            jax.ShapeDtypeStruct((targets, FULL) + shape, dtype),
            jax.ShapeDtypeStruct((NDP, lanes, span), jnp.float32),
            jax.ShapeDtypeStruct((NDP, 1, span), jnp.float32),
            jax.ShapeDtypeStruct((grains, GRAIN), jnp.float32),
        ],
        scratch_shapes=[
            pltpu.VMEM(shares.shape, dtype),
            pltpu.VMEM((targets, room) + shape, dtype),
            [pltpu.VMEM((targets // 2, room + min(SPARE, FULL - room)) + shape, dtype)] * 2,
            buffer(NDP, lanes),
            pltpu.VMEM((stored, lanes, 1), jnp.float32),
            buffer(NDP, 2),
            buffer(NDP, 2), buffer(listed, 2), buffer(NQ - 1, listed, 2), buffer(listed, 1), buffer(NDP, 1), buffer(NDP, 1),
            dma((2,)), dma((2, 2, targets // 2)), dma((2, 2, targets // 2)), dma((2, 2)), dma((2, 2, 2)), dma((3, 2)),
        ],
        compiler_params=pltpu.CompilerParams(
            collective_id=collective_id, has_side_effects=True, vmem_limit_bytes=VMEM_LIMIT
        ),
        cost_estimate=pl.CostEstimate(
            flops=2 * NDP * lanes * span * width,
            bytes_accessed=2 * (shares.size + 3 * targets * room * shape[0] * shape[1]),
            transcendentals=NDP * lanes * span,
        ),
    )(*tables, shares, centroids)


def on_device(embeddings, point_parent, parent_list, block_slots, centroids):
    y, z, c, q = (lax.axis_index(a) for a in ("y", "z", "core", "cand"))
    here = (y * NZ + z) * NC + c
    row_count, width = embeddings.shape
    stored = centroids.shape[0]
    listed = parent_list.shape[1]
    grains = row_count // GRAIN
    local = grains // NQ
    i32 = jnp.int32

    share = lax.dynamic_index_in_dim(embeddings.reshape(local, NQ, GRAIN, width), q, 1, keepdims=False)
    shares = lax.all_gather(share, ("z", "core"), axis=0, tiled=True)

    counts = jnp.sum((point_parent[:, None] == parent_list[here][None, :]).astype(i32), axis=0)
    counts = census(counts, 1)
    starts = jnp.cumsum(counts, axis=1) - counts
    begin = starts // GRAIN
    last = (starts + counts - 1) // GRAIN
    low = starts % GRAIN
    high = low + counts
    slots = jnp.take(block_slots, parent_list, axis=0)
    owner = slots // (stored * NQ)
    planes = jnp.arange(NQ, dtype=i32)

    def share_of(begin, last, plane):
        nearest = begin + (plane - begin) % NQ
        return nearest, (nearest <= last).astype(i32) + (nearest + NQ <= last).astype(i32)

    loads = share_of(begin[..., None], last[..., None], planes)[1]
    loads = jnp.broadcast_to(loads[:, :, None, :], (NDP, listed, 2, NQ)).reshape(NY, PER_Y * listed * 2, NQ)
    takers = jnp.swapaxes(owner, 2, 3).reshape(NY, PER_Y * listed * 2, NQ)
    takes = takers[..., None] == jnp.arange(NDP, dtype=i32)
    totals = jnp.einsum(
        "ymqj,ymp->yqjp", takes.astype(jnp.bfloat16), loads.astype(jnp.bfloat16), preferred_element_type=jnp.float32
    )
    paired = jnp.sum(totals.reshape(NY, NQ, NDP // NC, NC, NQ), axis=3)
    rooms = jnp.asarray(ROOMS[:-1], jnp.float32)
    size = jnp.sum(((jnp.max(paired) > 2 * rooms) | (jnp.max(totals) > rooms + SPARE)).astype(i32))
    room = jnp.asarray(ROOMS, i32)[size]

    mine = jnp.take(owner, q, axis=2) == here
    entry = jnp.any(mine, axis=2)
    chosen = lambda value: jnp.sum(jnp.where(entry, value, 0), axis=1)
    served = jnp.any(entry, axis=1)
    serve_low, serve_high, serve_begin = chosen(low), chosen(high), chosen(begin)
    serve_last = jnp.where(served, chosen(last), -1)
    serve_block = jnp.sum(jnp.where(mine, jnp.take(slots, q, axis=2) % stored, 0), axis=(1, 2))
    grouped = served.reshape(NY, PER_Y).astype(i32)
    many = jnp.sum(grouped, axis=1)
    rank = jnp.where(
        grouped > 0, jnp.cumsum(grouped, axis=1) - 1, many[:, None] + jnp.cumsum(1 - grouped, axis=1) - 1
    )
    around = jnp.arange(PER_Y, dtype=i32)
    order = jnp.sum(jnp.where(rank[:, :, None] == around, around[None, :, None], 0), axis=1).reshape(-1)
    serving = (serve_block, serve_low, serve_high, order, many)

    _, landing = share_of(serve_begin[:, None], serve_last[:, None], planes)
    landing = landing.reshape(NY, PER_Y, NQ)
    base = (jnp.cumsum(landing, axis=1) - landing).reshape(NDP, NQ)
    step = jnp.arange(SPAN, dtype=i32)
    grain = serve_begin[:, None] + step
    plane = grain % NQ
    within = jnp.sum(jnp.where(plane[..., None] == planes, base[:, None, :], 0), axis=2) + step // NQ
    real = grain <= serve_last[:, None]
    within = jnp.where(real, within, within[:, :1])
    plane = jnp.where(real, plane, plane[:, :1])
    within = jnp.where(within < room, within, 2 * room + SPARE - 1 - within)
    within = jnp.where(served[:, None], within, 0)

    own = lambda value: lax.dynamic_index_in_dim(value, here, 0, keepdims=False)
    dps = jnp.arange(NDP, dtype=i32)
    depth_order = dps.reshape(NY, NZ, NC).transpose(0, 2, 1).reshape(-1)
    own_owner = own(jnp.take(owner, q, axis=2))
    pick = jnp.sum(
        jnp.where(own_owner[None] == depth_order[:, None, None], jnp.arange(listed, dtype=i32)[None, :, None], 0),
        axis=(1, 2),
    )
    deep = lambda index: by_depth(index // PER_Y, index // NC % NZ, index % NC)

    of_y = lambda value: lax.dynamic_index_in_dim(value.reshape((NY, PER_Y) + value.shape[1:]), y, 0, keepdims=False)
    target = (jnp.arange(NY, dtype=i32)[:, None] * NZ + z) * NC + jnp.arange(NC, dtype=i32)
    hit = jnp.any(of_y(owner) == target[:, :, None, None, None, None], axis=-1)
    sent = lambda value: jnp.sum(jnp.where(hit, of_y(value)[:, :, None], 0), axis=3)
    nearest, sending = share_of(sent(begin), jnp.where(jnp.any(hit, axis=3), sent(last), -1), q)
    place = jnp.cumsum(sending, axis=2) - sending
    places = jnp.arange(FULL, dtype=i32)
    straight = (jnp.arange(NC, dtype=i32) == c)[None, :, None, None]
    picks = 0
    for slot in range(2):
        spot = place + slot
        spot = jnp.where(straight, jnp.where(spot < room, spot, -1), jnp.where(spot < room, -1, 2 * room - 1 - spot))
        here_now = (spot[..., None] == places) & (sending[..., None] > slot)
        which = around[:, None] * local + nearest // NQ + slot
        picks = picks + jnp.sum(jnp.where(here_now, which[..., None], 0), axis=(1, 2))
    tables = (picks.reshape(-1), (plane * FULL + within).reshape(-1), serve_block)
    tables += (deep(own_owner[:, 0]), deep(own_owner[:, 1]), pick, own(begin), own(low), own(high))
    tables = lax.optimization_barrier(tables)

    def finish(most, collective_id, shares, centroids, *tables):
        rows, logits, norms, log_norms = serve(most, collective_id, grains, shares, centroids, *tables)
        rows = rows.reshape(NY, NQ, FULL, GRAIN, width)
        used = min(most + SPARE, FULL)
        return update(rows, tables[1], serving, used, centroids, logits, norms), log_norms

    branches = [functools.partial(finish, most, 2 + n) for n, most in enumerate(ROOMS)]
    updated, log_norms = lax.switch(size, branches, shares, centroids, *tables)
    return updated, log_norms.reshape(row_count)


def solution(mesh):
    split = Mesh(mesh.devices.reshape(NY, NZ, NC, NQ), ("y", "z", "core", "cand"))
    dp = ("y", "z", "core")
    every = dp + ("cand",)
    return jax.shard_map(
        on_device,
        mesh=split,
        in_specs=(P(dp, None), P(dp), P(), P(), P(every, None, None)),
        out_specs=(P(every, None, None), P(dp)),
        check_vma=False,
    )
```
